128 devices in a mesh: dp: 16 (over y, z), fsdp: 8 (over x, core).
Axes of the slice: x: 4, y: 4, z: 4, core: 2. Of those that a mesh axis runs over, the one named last changes fastest.
Arguments:
- head_output: bfloat16 [262144, 2048], P(('dp', 'fsdp')), may hold values from -6 to 6
- router_logits: float32 [262144], P(('dp', 'fsdp')), may hold values from -8 to 8
- chosen_slots: int32 [128, 512], P(('dp', 'fsdp')), may hold values from 0 to 2047, as said below
- block_owner: int32 [128, 16], P(('dp', 'fsdp')), may hold values from 0 to 16, as said below
- out_weight: bfloat16 [2048, 4096], P('fsdp'), may hold values from -0.125 to 0.125
- cotangent: bfloat16 [32768, 4096], P(('dp', 'fsdp')), may hold values from -6 to 6
Outputs:
- update: bfloat16 [32768, 4096], P(('dp', 'fsdp'))
- grad_context: bfloat16 [65536, 2048], P(('dp', 'fsdp'))
- grad_logit: bfloat16 [65536], P(('dp', 'fsdp'))
- grad_weight: float32 [2048, 4096], P('fsdp')
The draws below stay inside these ranges and needn't reach their ends.
Inputs may be any that keep to these rules, and one draw needn't show every extreme that they name: `chosen_slots`: in each device's row the first (used blocks) * 32 entries are distinct tokens in ascending order; the remaining entries are other distinct tokens of the device and are not read. `block_owner`: used blocks precede unused ones. Within one fsdp index every dp index is owner of exactly 8 blocks, a device gives at most one block to any one owner, and some device has all 16 blocks used.
All inputs are finite; a program needn't handle non-finite values.
Results may differ from the reference program's by a relative error of at most 0.025.
Values may be sent and summed in bfloat16 or wider, within the bound.
No kernel may reach another device: no remote copies, remote signals or barrier semaphores. Data moves between devices by JAX's collectives and lax.ppermute only.
A program may use at most 192 MiB of HBM per device.

```python
import math
import jax
import jax.numpy as jnp
from jax import lax

D = 4096
HV = 2048
BLK = 32
RECV = 8
MOST = 16
SLOTS = 512
TOK_DEV = 2048
TOKENS = 262144
CHOSEN = 32768
N_DP = 16
N_FSDP = 8
DEVICES = 128


def block_counts(key):

    def column(column_id):
        column_key = jax.random.fold_in(key, column_id)
        ordering = jax.random.permutation(column_key, N_DP)
        swings = jax.random.randint(jax.random.fold_in(column_key, 7), (N_DP // 2,), 0, RECV + 1)
        swings = swings.at[0].set(RECV)
        shift_by = jnp.concatenate([swings, -swings])
        return jnp.zeros((N_DP,), jnp.int32).at[ordering].set(RECV + shift_by)
    return jax.vmap(column)(jnp.arange(N_FSDP)).T


def draw_block_owner(key, part):
    counts_used = block_counts(key)
    first_block = jnp.cumsum(counts_used, axis=0) - counts_used
    block_ids = jnp.arange(MOST, dtype=jnp.int32)
    counter = first_block[:, :, None] + block_ids[None, None, :]
    owners = jnp.where(block_ids[None, None, :] < counts_used[:, :, None], counter % N_DP, N_DP)
    return owners.reshape(DEVICES, MOST).astype(jnp.int32)


def draw_chosen_slots(key, part):
    counts_used = block_counts(key)
    key = jax.random.fold_in(key, 5)
    live_rows = counts_used.reshape(-1) * BLK

    def device_row(device_id, live_count):
        ranking = jax.random.permutation(jax.random.fold_in(key, device_id), TOK_DEV)[:SLOTS]
        places = jnp.arange(SLOTS, dtype=jnp.int32)
        sort_keys = jnp.where(places < live_count, ranking, TOK_DEV + ranking)
        return (jnp.sort(sort_keys) % TOK_DEV).astype(jnp.int32)
    return jax.vmap(device_row)(jnp.arange(DEVICES), live_rows)


def block_scale(stream_key, dims, split, least, largest):
    gain, own = 1.0, jax.random.fold_in(stream_key, 6)
    for dim, blocks in split:
        steps = jnp.exp(jax.random.uniform(jax.random.fold_in(own, dim), (blocks,), jnp.float32, least / len(split), largest / len(split)))
        gain = gain * jnp.repeat(steps, dims[dim] // blocks).reshape([-1 if axis == dim else 1 for axis in range(len(dims))])
    return gain


def normal_values(rng, shape, deviation, bound, split=(), kind=jnp.bfloat16):
    level = block_scale(rng, shape, split, -0.22, 0.18) if split else 1.0
    entries = jax.random.normal(rng, shape, jnp.float32) * deviation * level
    return jnp.minimum(jnp.maximum(entries, -bound), bound).astype(kind)


def setup_inputs(seed: int = 0) -> dict:
    key_of = jax.random.split(jax.random.key(seed), 7)
    head_output = normal_values(key_of[0], (TOKENS, HV), 1.0, 6.0, ((0, 128),))
    router_logits = normal_values(key_of[1], (TOKENS,), 2.0, 8.0, ((0, 128),), jnp.float32)
    chosen_slots = draw_chosen_slots(jax.random.fold_in(key_of[6], 71), 0)
    block_owner = draw_block_owner(jax.random.fold_in(key_of[6], 71), 0)
    out_weight = normal_values(key_of[4], (HV, D), HV ** -0.5, 0.125, ((0, 8),))
    cotangent = normal_values(key_of[5], (CHOSEN, D), 1.0, 6.0, ((0, 128),))
    return dict(head_output=head_output, router_logits=router_logits, chosen_slots=chosen_slots, block_owner=block_owner, out_weight=out_weight, cotangent=cotangent)


def rounded(values):
    return lax.optimization_barrier(values.astype(jnp.bfloat16)).astype(jnp.float32)

def placed_index(block_owner):
    owners = block_owner.reshape(N_DP, N_FSDP, MOST)
    targets = jnp.arange(N_DP, dtype=jnp.int32)
    sending = jnp.any(owners[:, :, :, None] == targets[None, None, None, :], axis=2).astype(jnp.int32)
    earlier = jnp.cumsum(sending, axis=0) - sending
    used = owners < N_DP
    owner_safe = jnp.where(used, owners, 0).astype(jnp.int32)
    ranking = jnp.take_along_axis(earlier, owner_safe, axis=2)
    columns = jnp.arange(N_FSDP, dtype=jnp.int32)[None, :, None]
    position = (owner_safe * N_FSDP + columns) * RECV + ranking
    return jnp.where(used, position, N_DP * N_FSDP * RECV).reshape(-1).astype(jnp.int32)

def reference(head_output, router_logits, chosen_slots, block_owner, out_weight, cotangent):
    device_count = N_DP * N_FSDP
    per_device = head_output.reshape(device_count, TOK_DEV, HV)
    logit_rows = router_logits.reshape(device_count, TOK_DEV)
    picked_rows = jax.vmap(lambda table, where: table[where])(per_device, chosen_slots)
    picked_logits = jax.vmap(lambda table, where: table[where])(logit_rows, chosen_slots)
    gating = jax.nn.sigmoid(picked_logits).astype(jnp.bfloat16)
    target = placed_index(block_owner)
    balanced = jnp.zeros((device_count * RECV, BLK, HV), jnp.bfloat16)
    balanced = balanced.at[target].set(picked_rows.reshape(device_count * MOST, BLK, HV), mode='drop')
    balanced = balanced.reshape(CHOSEN, HV)
    balanced_gate = jnp.zeros((device_count * RECV, BLK), jnp.bfloat16)
    balanced_gate = balanced_gate.at[target].set(gating.reshape(device_count * MOST, BLK), mode='drop')
    balanced_gate = balanced_gate.reshape(CHOSEN)
    projected = jnp.dot(balanced, out_weight, preferred_element_type=jnp.float32)
    gate_wide = balanced_gate.astype(jnp.float32)
    update = (gate_wide[:, None] * projected).astype(jnp.bfloat16)
    weighted = (gate_wide[:, None] * cotangent.astype(jnp.float32)).astype(jnp.bfloat16)
    processed_grad = lax.dot_general(weighted, out_weight, (((1,), (1,)), ((), ())), preferred_element_type=jnp.float32).astype(jnp.bfloat16)
    inner_sum = lax.optimization_barrier(jnp.sum(cotangent.astype(jnp.float32) * projected, axis=1))
    logit_grad = (gate_wide * (1.0 - gate_wide) * inner_sum).astype(jnp.bfloat16)
    padded_grad = jnp.concatenate([processed_grad.reshape(device_count * RECV, BLK, HV), jnp.zeros((1, BLK, HV), jnp.bfloat16)], axis=0)
    padded_logit = jnp.concatenate([logit_grad.reshape(device_count * RECV, BLK), jnp.zeros((1, BLK), jnp.bfloat16)], axis=0)
    grad_context = padded_grad[target].reshape(device_count * SLOTS, HV)
    grad_logit = padded_logit[target].reshape(device_count * SLOTS)
    grad_scale = 1.0 / math.sqrt(CHOSEN)
    grouped_rows = balanced.reshape(N_DP, N_FSDP, RECV * BLK, HV)
    grouped_weighted = weighted.reshape(N_DP, N_FSDP, RECV * BLK, D)

    def group_sum(running, group_id):

        def device_sum(inner_running, member):
            partial_term = lax.dot_general(grouped_rows[group_id, member], grouped_weighted[group_id, member], (((0,), (0,)), ((), ())), preferred_element_type=jnp.float32) * grad_scale
            return (inner_running + rounded(partial_term), None)
        group_total, _ = lax.scan(device_sum, jnp.zeros((HV, D), jnp.float32), jnp.arange(N_FSDP))
        return (running + rounded(group_total), None)
    grad_weight, _ = lax.scan(group_sum, jnp.zeros((HV, D), jnp.float32), jnp.arange(N_DP))
    return (update, grad_context, grad_logit, grad_weight)
```

```python
import math

import jax
import jax.numpy as jnp
from jax import lax
from jax.experimental import pallas as pl
from jax.experimental.pallas import tpu as pltpu
from jax.sharding import PartitionSpec as P

EXTRA = 128
VMEM_LIMIT = 56 * 1024 * 1024


def params():
    return pltpu.CompilerParams(vmem_limit_bytes=VMEM_LIMIT)


def pick_body(width, token_ref, head_ref, extra_ref, out_ref, onehot_ref):
    step = pl.program_id(0)
    columns = head_ref.shape[1]

    @pl.when(step == 0)
    def _():
        tokens = lax.broadcasted_iota(jnp.int32, onehot_ref.shape, 1)
        onehot_ref[...] = (token_ref[...] == tokens).astype(jnp.bfloat16)
        out_ref[:, width:] = jnp.dot(
            onehot_ref[...], extra_ref[...], preferred_element_type=jnp.float32
        ).astype(jnp.bfloat16)

    out_ref[:, pl.ds(pl.multiple_of(step * columns, columns), columns)] = jnp.dot(
        onehot_ref[...], head_ref[...], preferred_element_type=jnp.float32
    ).astype(jnp.bfloat16)


def pick_rows(tokens, head, extra):
    rows = tokens.shape[0]
    count, width = head.shape
    columns = 256
    return pl.pallas_call(
        lambda *refs: pick_body(width, *refs),
        out_shape=jax.ShapeDtypeStruct((rows, width + EXTRA), jnp.bfloat16),
        grid=(width // columns,),
        in_specs=[
            pl.BlockSpec((rows, 1), lambda n: (0, 0)),
            pl.BlockSpec((count, columns), lambda n: (0, n)),
            pl.BlockSpec((count, EXTRA), lambda n: (0, 0)),
        ],
        out_specs=pl.BlockSpec((rows, width + EXTRA), lambda n: (0, 0)),
        scratch_shapes=[pltpu.VMEM((rows, count), jnp.bfloat16)],
        compiler_params=params(),
        cost_estimate=pl.CostEstimate(
            flops=2 * rows * count * width,
            bytes_accessed=2 * (count * width + rows * width),
            transcendentals=0,
        ),
        name="pick_rows",
    )(tokens[:, None], head, extra)


def move_body(width, index_ref, source_ref, out_ref):
    blocks = source_ref.shape[0]
    for slot in range(out_ref.shape[0]):
        block = index_ref[slot]

        @pl.when(block < blocks)
        def _():
            out_ref[slot] = source_ref[jnp.minimum(block, blocks - 1), :, :width]

        @pl.when(block >= blocks)
        def _():
            out_ref[slot] = jnp.zeros(out_ref.shape[1:], out_ref.dtype)


def move_blocks(source, index, width):
    blocks, rows, _ = source.shape
    copies = index.shape[0]
    return pl.pallas_call(
        lambda *refs: move_body(width, *refs),
        out_shape=jax.ShapeDtypeStruct((copies, rows, width), source.dtype),
        in_specs=[
            pl.BlockSpec(memory_space=pltpu.SMEM),
            pl.BlockSpec(memory_space=pltpu.VMEM),
        ],
        out_specs=pl.BlockSpec(memory_space=pltpu.VMEM),
        compiler_params=params(),
        cost_estimate=pl.CostEstimate(
            flops=0, bytes_accessed=4 * copies * rows * width, transcendentals=0
        ),
        name="move_blocks",
    )(index, source)


def project_body(shards, width, *refs):
    place_ref, rows_ref, cot_ref = refs[:3]
    weights = refs[3 : 3 + shards + 2]
    update_ref, grad_ref, lhs_ref, weight_ref, total_ref, inner_ref = refs[3 + shards + 2 :]
    step, steps = pl.program_id(0), pl.num_programs(0)
    part = width // shards

    @pl.when(step == 0)
    def _():
        total_ref[...] = jnp.zeros_like(total_ref)
        inner_ref[...] = jnp.zeros_like(inner_ref)
        for i in range(shards):
            start = pl.multiple_of(place_ref[i] * part, part)
            lhs_ref[:, i * part : (i + 1) * part] = rows_ref[:, pl.ds(start, part)]

    for i in range(shards - 2):
        weight_ref[i * part : (i + 1) * part, :] = weights[i][...]
    for i in range(2):
        at = (shards - 2 + i) * part

        @pl.when(step < steps // 2)
        def _():
            weight_ref[at : at + part, :] = weights[shards - 2 + 2 * i][...]

        @pl.when(step >= steps // 2)
        def _():
            weight_ref[at : at + part, :] = weights[shards - 1 + 2 * i][...]

    weight = weight_ref[...]
    gate = rows_ref[:, width : width + 1].astype(jnp.float32)
    projected = jnp.dot(lhs_ref[...], weight, preferred_element_type=jnp.float32)
    update_ref[...] = (gate * projected).astype(jnp.bfloat16)
    cot = cot_ref[...].astype(jnp.float32)
    inner_ref[...] += cot * projected
    weighted = (gate * cot).astype(jnp.bfloat16)
    total_ref[...] += lax.dot_general(
        weighted, weight, (((1,), (1,)), ((), ())), preferred_element_type=jnp.float32
    )

    @pl.when(step == steps - 1)
    def _():
        for i in range(shards):
            start = pl.multiple_of(place_ref[i] * part, part)
            grad_ref[:, pl.ds(start, part)] = total_ref[:, i * part : (i + 1) * part].astype(jnp.bfloat16)
        inner = jnp.sum(inner_ref[...], axis=1, keepdims=True)
        logit = gate * (1.0 - gate) * inner
        grad_ref[:, width:] = jnp.broadcast_to(logit, (logit.shape[0], EXTRA)).astype(jnp.bfloat16)


def project(rows, cotangent, places, weights):
    count, wide = rows.shape
    width = wide - EXTRA
    model = cotangent.shape[1]
    shards = len(weights) - 2
    part = width // shards
    columns = 512
    steps = model // columns
    whole = pl.BlockSpec((part, columns), lambda n: (0, n))
    left = pl.BlockSpec((part, columns), lambda n: (0, jnp.minimum(n, steps // 2 - 1)))
    right = pl.BlockSpec((part, columns), lambda n: (0, jnp.maximum(n - steps // 2, 0)))
    return pl.pallas_call(
        lambda *refs: project_body(shards, width, *refs),
        out_shape=(
            jax.ShapeDtypeStruct((count, model), jnp.bfloat16),
            jax.ShapeDtypeStruct((count, wide), jnp.bfloat16),
        ),
        grid=(steps,),
        in_specs=[
            pl.BlockSpec(memory_space=pltpu.SMEM),
            pl.BlockSpec((count, wide), lambda n: (0, 0)),
            pl.BlockSpec((count, columns), lambda n: (0, n)),
        ]
        + [whole] * (shards - 2)
        + [left, right] * 2,
        out_specs=(
            pl.BlockSpec((count, columns), lambda n: (0, n)),
            pl.BlockSpec((count, wide), lambda n: (0, 0)),
        ),
        scratch_shapes=[
            pltpu.VMEM((count, width), jnp.bfloat16),
            pltpu.VMEM((width, columns), jnp.bfloat16),
            pltpu.VMEM((count, width), jnp.float32),
            pltpu.VMEM((count, columns), jnp.float32),
        ],
        compiler_params=params(),
        cost_estimate=pl.CostEstimate(
            flops=4 * count * width * model,
            bytes_accessed=2 * (model * (width + 2 * count) + 2 * count * wide),
            transcendentals=0,
        ),
        name="project",
    )(places, rows, cotangent, *weights)


def place_body(first_ref, second_ref, out_ref):
    side, _, halves, _, _, columns = first_ref.shape
    half = out_ref.shape[1] // halves
    for h in range(halves):
        for k in range(side):
            left = h * half + k * columns
            right = left + half // 2
            out_ref[:, left : left + columns] = first_ref[k, 0, h, 0].astype(jnp.float32)
            out_ref[:, right : right + columns] = second_ref[0, k, h, 0].astype(jnp.float32)


def place_blocks(pieces):
    side, _, halves, _, rows, columns = pieces.shape
    model = halves * 2 * side * columns
    return pl.pallas_call(
        place_body,
        out_shape=jax.ShapeDtypeStruct((side * rows, model), jnp.float32),
        grid=(side,),
        in_specs=[
            pl.BlockSpec((side, 1, halves, 1, rows, columns), lambda r: (0, r, 0, 0, 0, 0)),
            pl.BlockSpec((1, side, halves, 1, rows, columns), lambda r: (r, 0, 0, 1, 0, 0)),
        ],
        out_specs=pl.BlockSpec((rows, model), lambda r: (r, 0)),
        compiler_params=params(),
        cost_estimate=pl.CostEstimate(
            flops=0, bytes_accessed=6 * side * rows * model, transcendentals=0
        ),
        name="place_blocks",
    )(pieces, pieces)


def at(array, index, axis=0):
    return lax.dynamic_index_in_dim(array, index, axis, keepdims=False)


def on_device(head_output, router_logits, chosen_slots, block_owner, out_weight, cotangent):
    n_dp, n_fsdp = lax.axis_size("dp"), lax.axis_size("fsdp")
    dp, fsdp = lax.axis_index("dp"), lax.axis_index("fsdp")
    side, chips = math.isqrt(n_dp), n_fsdp // 2
    y, z = dp // side, dp % side
    chip, core = fsdp // 2, fsdp % 2

    def along_x(value, ahead):
        return lax.ppermute(value, "fsdp", [(f, (f + 2 * ahead) % n_fsdp) for f in range(n_fsdp)])

    def along_y(value, ahead):
        return lax.ppermute(value, "dp", [(d, (d + side * ahead) % n_dp) for d in range(n_dp)])

    def along_z(value, ahead):
        return lax.ppermute(
            value, "dp", [(d, d // side * side + (d + ahead) % side) for d in range(n_dp)]
        )

    def to_partner(value):
        return lax.ppermute(value, "fsdp", [(f, f ^ 1) for f in range(n_fsdp)])

    slots = chosen_slots.shape[1]
    blocks = block_owner.shape[1]
    block = slots // blocks
    tokens, width = head_output.shape
    shard, model = out_weight.shape
    rows = cotangent.shape[0]
    receive = rows // block
    scale = 1.0 / math.sqrt(rows * n_dp * n_fsdp)
    half = model // 2
    owner = block_owner[0]

    below = along_x(out_weight, 1)
    above = along_x(out_weight, -1)
    far_left = along_x(below[:, :half], 1)
    far_right = along_x(above[:, half:], -1)
    mine = (out_weight, below, above, far_left, far_right)
    theirs = tuple(to_partner(w) for w in mine)
    weights = mine[:3] + theirs[:3] + mine[3:] + theirs[3:]
    near = (chip, (chip + chips - 1) % chips, (chip + 1) % chips)
    places = [2 * c + core for c in near] + [2 * c + 1 - core for c in near]
    opposite = 2 * ((chip + 2) % chips)
    places = jnp.stack(places + [opposite + core, opposite + 1 - core]).astype(jnp.int32)

    own_cot = lax.dynamic_slice(cotangent, (0, core * half), (rows, half))
    partner_cot = to_partner(lax.dynamic_slice(cotangent, (0, (1 - core) * half), (rows, half)))

    peers = jnp.arange(n_dp, dtype=jnp.int32)
    match = owner[None, :] == peers[:, None]
    listed = chosen_slots[0].reshape(1, blocks, block) + 1
    token = jnp.sum(jnp.where(match[:, :, None], listed, 0), axis=1).reshape(-1) - 1
    gates = jax.nn.sigmoid(router_logits).astype(jnp.bfloat16)
    lane = lax.broadcasted_iota(jnp.int32, (tokens, EXTRA), 1)
    extra = jnp.where(lane == 0, gates[:, None], (lane == 1).astype(jnp.bfloat16))
    send = pick_rows(token, head_output, extra).reshape(n_dp, block, width + EXTRA)
    got = lax.all_to_all(send, "dp", split_axis=0, concat_axis=0, tiled=True)

    incoming = (got[:, 0, width + 1] > 0.5).astype(jnp.int32)
    position = jnp.cumsum(incoming) - 1
    ids = jnp.arange(receive, dtype=jnp.int32)
    source = jnp.sum(
        jnp.where((position[None, :] == ids[:, None]) & (incoming[None, :] > 0), peers[None, :], 0),
        axis=1,
    )
    held = move_blocks(got, source, width + EXTRA).reshape(rows, width + EXTRA)

    both = jnp.concatenate([held, to_partner(held)], axis=0)
    both_cot = jnp.concatenate([own_cot, partner_cot], axis=0)
    gate = both[:, width].astype(jnp.float32)
    weighted = (gate[:, None] * both_cot.astype(jnp.float32)).astype(jnp.bfloat16)
    both_rows = both[:, :width]
    part = half // (2 * side)
    cut = width // 2

    def term(first, index):
        columns = lax.dynamic_slice(weighted, (0, first + index % side * part), (2 * rows, part))
        product = lax.dot_general(
            both_rows, columns, (((0,), (0,)), ((), ())), preferred_element_type=jnp.float32
        )
        return product * scale

    def wide(value):
        return value.astype(jnp.float32)

    def narrow(value):
        return value.astype(jnp.bfloat16)

    far_y, far_z = narrow(term(0, y + 2)), narrow(term(half // 2, z + 2))
    up_y, up_z = along_y(far_y[:cut], 1), along_z(far_z[:cut], 1)
    down_y, down_z = along_y(far_y[cut:], -1), along_z(far_z[cut:], -1)

    def onward(value, got, upper):
        if upper:
            return narrow(jnp.concatenate([value[:cut] + wide(got), value[cut:]], axis=0))
        return narrow(jnp.concatenate([value[:cut], value[cut:] + wide(got)], axis=0))

    from_y = along_y(onward(term(0, y + 1), up_y, True), 1)
    from_z = along_z(onward(term(half // 2, z + 1), up_z, True), 1)
    to_y = along_y(onward(term(0, y + side - 1), down_y, False), -1)
    to_z = along_z(onward(term(half // 2, z + side - 1), down_z, False), -1)
    sum_y = narrow(term(0, y) + wide(from_y) + wide(to_y))
    sum_z = narrow(term(half // 2, z) + wide(from_z) + wide(to_z))

    share = shard // side

    def exchange(value, axis, place, along):
        count = value.shape[axis]
        total = wide(at(value, place, axis))
        for ahead in range(1, count):
            total += wide(along(at(value, (place + ahead) % count, axis), ahead))
        return narrow(total)

    sum_y = exchange(sum_y.reshape(n_fsdp, side, share, part), 1, z, along_z)
    sum_z = exchange(sum_z.reshape(n_fsdp, side, share, part), 1, y, along_y)
    sums = jnp.stack([sum_y, sum_z]).reshape(2, chips, 2, share, part)
    sums = exchange(sums, 1, chip, along_x)
    keep, take = at(sums, core, 1), to_partner(at(sums, 1 - core, 1))
    first = core == 0
    piece = jnp.stack([jnp.where(first, keep, take), jnp.where(first, take, keep)])
    pieces = lax.all_to_all(
        jnp.broadcast_to(piece[None], (n_dp,) + piece.shape), "dp", split_axis=0, concat_axis=0, tiled=True
    )
    grad_weight = place_blocks(pieces.reshape((side, side) + piece.shape))

    update, grads = project(held, cotangent, places, weights)
    back = move_blocks(
        grads.reshape(receive, block, width + EXTRA), jnp.clip(position, 0, receive - 1), width + EXTRA
    )
    returned = lax.all_to_all(back, "dp", split_axis=0, concat_axis=0, tiled=True)
    grad_context = move_blocks(returned, owner, width).reshape(slots, width)
    logit_blocks = returned[:, :, width]
    grad_logit = jnp.sum(jnp.where(match[:, :, None], logit_blocks[:, None, :], 0), axis=0).reshape(-1)
    return (update, grad_context, narrow(grad_logit), grad_weight)


def solution(mesh):
    placed = (
        P(("dp", "fsdp"), None),
        P(("dp", "fsdp")),
        P(("dp", "fsdp"), None),
        P(("dp", "fsdp"), None),
        P("fsdp", None),
        P(("dp", "fsdp"), None),
    )
    return jax.shard_map(
        on_device,
        mesh=mesh,
        in_specs=placed,
        out_specs=(
            P(("dp", "fsdp"), None),
            P(("dp", "fsdp"), None),
            P(("dp", "fsdp")),
            P("fsdp", None),
        ),
        check_vma=False,
    )
```

```python
import math

import jax
import jax.numpy as jnp
from jax import lax
from jax.experimental import pallas as pl
from jax.experimental.pallas import tpu as pltpu
from jax.sharding import PartitionSpec as P

EXTRA = 128
MIB = 1024 * 1024
NO_COST = pl.CostEstimate(flops=0, bytes_accessed=0, transcendentals=0)


def params(limit=24):
    return pltpu.CompilerParams(vmem_limit_bytes=limit * MIB)


def after(value, *others):
    return lax.optimization_barrier((value, others))[0]


def pick_body(width, owner_ref, listed_ref, logit_ref, head_ref, out_ref, onehot_ref):
    step = pl.program_id(0)
    columns = head_ref.shape[1]
    rows, count = onehot_ref.shape
    blocks = owner_ref.shape[0]
    block = rows // blocks

    @pl.when(step == 0)
    def _():
        lane = lax.broadcasted_iota(jnp.int32, (block, EXTRA), 1)
        tokens = lax.broadcasted_iota(jnp.int32, (block, count), 1)
        for peer in range(rows // block):
            found = jnp.int32(blocks)
            for b in range(blocks):
                found = jnp.where(owner_ref[b] == peer, b, found)
            there = found < blocks
            start = pl.multiple_of(jnp.minimum(found, blocks - 1) * block, block)
            listed = jnp.where(there, listed_ref[pl.ds(start, block), :], -1)
            hit = listed == tokens
            span = slice(peer * block, (peer + 1) * block)
            onehot_ref[span, :] = hit.astype(jnp.bfloat16)
            logit = jnp.sum(jnp.where(hit, logit_ref[...], 0.0), axis=1, keepdims=True)
            mark = jnp.where(there, 1.0, 0.0)
            out_ref[span, width:] = jnp.where(lane == 0, jax.nn.sigmoid(logit), mark).astype(jnp.bfloat16)

    out_ref[:, pl.ds(pl.multiple_of(step * columns, columns), columns)] = jnp.dot(
        onehot_ref[...], head_ref[...], preferred_element_type=jnp.float32
    ).astype(jnp.bfloat16)


def pick_rows(owner, listed, logits, head):
    rows = listed.shape[0]
    count, width = head.shape
    columns = 512
    return pl.pallas_call(
        lambda *refs: pick_body(width, *refs),
        out_shape=jax.ShapeDtypeStruct((rows, width + EXTRA), jnp.bfloat16),
        grid=(width // columns,),
        in_specs=[
            pl.BlockSpec(memory_space=pltpu.SMEM),
            pl.BlockSpec((rows, 1), lambda n: (0, 0)),
            pl.BlockSpec((1, count), lambda n: (0, 0)),
            pl.BlockSpec((count, columns), lambda n: (0, n)),
        ],
        out_specs=pl.BlockSpec((rows, width + EXTRA), lambda n: (0, 0)),
        scratch_shapes=[pltpu.VMEM((rows, count), jnp.bfloat16)],
        compiler_params=params(56),
        cost_estimate=NO_COST,
        name="pick_rows",
    )(owner, listed, logits, head)


def move_body(width, index_ref, source_ref, out_ref):
    blocks = source_ref.shape[0]
    for slot in range(out_ref.shape[0]):
        block = index_ref[slot]

        @pl.when(block < blocks)
        def _():
            out_ref[slot] = source_ref[jnp.minimum(block, blocks - 1), :, :width]

        @pl.when(block >= blocks)
        def _():
            out_ref[slot] = jnp.zeros(out_ref.shape[1:], out_ref.dtype)


def move_blocks(source, index, width):
    blocks, rows, _ = source.shape
    copies = index.shape[0]
    return pl.pallas_call(
        lambda *refs: move_body(width, *refs),
        out_shape=jax.ShapeDtypeStruct((copies, rows, width), source.dtype),
        in_specs=[
            pl.BlockSpec(memory_space=pltpu.SMEM),
            pl.BlockSpec(memory_space=pltpu.VMEM),
        ],
        out_specs=pl.BlockSpec(memory_space=pltpu.VMEM),
        compiler_params=params(),
        cost_estimate=NO_COST,
        name="move_blocks",
    )(index, source)


def project_body(width, slot_ref, rows_ref, weight_ref, cot_ref, update_ref, back_ref, total_ref, inner_ref):
    step, steps = pl.program_id(0), pl.num_programs(0)

    @pl.when(step == 0)
    def _():
        total_ref[...] = jnp.zeros_like(total_ref)
        inner_ref[...] = jnp.zeros_like(inner_ref)

    weight = weight_ref[...]
    gate = rows_ref[:, width : width + 1].astype(jnp.float32)
    projected = jnp.dot(rows_ref[:, :width], weight, preferred_element_type=jnp.float32)
    update_ref[...] = (gate * projected).astype(jnp.bfloat16)
    cot = cot_ref[...].astype(jnp.float32)
    inner_ref[...] += cot * projected
    weighted = (gate * cot).astype(jnp.bfloat16)
    total_ref[...] += lax.dot_general(
        weighted, weight, (((1,), (1,)), ((), ())), preferred_element_type=jnp.float32
    )

    @pl.when(step == steps - 1)
    def _():
        inner = jnp.sum(inner_ref[...], axis=1, keepdims=True)
        inner_ref[:, :EXTRA] = jnp.broadcast_to(gate * (1.0 - gate) * inner, (gate.shape[0], EXTRA))
        block = back_ref.shape[1]
        for peer in range(back_ref.shape[0]):
            start = pl.multiple_of(slot_ref[peer] * block, block)
            back_ref[peer, :, :width] = total_ref[pl.ds(start, block), :].astype(jnp.bfloat16)
            back_ref[peer, :, width:] = inner_ref[pl.ds(start, block), :EXTRA].astype(jnp.bfloat16)


def project(rows, weight, cotangent, slots, block):
    count, wide = rows.shape
    width, model = weight.shape
    columns = 512
    return pl.pallas_call(
        lambda *refs: project_body(width, *refs),
        out_shape=(
            jax.ShapeDtypeStruct((count, model), jnp.bfloat16),
            jax.ShapeDtypeStruct((slots.shape[0], block, wide), jnp.bfloat16),
        ),
        grid=(model // columns,),
        in_specs=[
            pl.BlockSpec(memory_space=pltpu.SMEM),
            pl.BlockSpec((count, wide), lambda n: (0, 0)),
            pl.BlockSpec((width, columns), lambda n: (0, n)),
            pl.BlockSpec((count, columns), lambda n: (0, n)),
        ],
        out_specs=(
            pl.BlockSpec((count, columns), lambda n: (0, n)),
            pl.BlockSpec((slots.shape[0], block, wide), lambda n: (0, 0, 0)),
        ),
        scratch_shapes=[
            pltpu.VMEM((count, width), jnp.float32),
            pltpu.VMEM((count, columns), jnp.float32),
        ],
        compiler_params=params(56),
        cost_estimate=NO_COST,
        name="project",
    )(slots, rows, weight, cotangent)


def place_body(side, spot_ref, *refs):
    out_ref = refs[-1]
    rows, columns = refs[0].shape[2:]
    across = out_ref.shape[1] // 2
    for which in range(2):
        line, cross = spot_ref[1 - which], spot_ref[which]
        for j in range(side):
            array = refs[which * side + j]
            place = (cross - j + side) % side * columns + which * across
            for k in range(side):
                top = (line - k + side) % side * rows
                out_ref[pl.ds(pl.multiple_of(top, rows), rows), pl.ds(pl.multiple_of(place, columns), columns)] = array[
                    k, 0
                ].astype(jnp.float32)


def place_blocks(spot, first, second):
    side, halves, rows, columns = first[0].shape
    model = halves * 2 * side * columns
    block = pl.BlockSpec((side, 1, rows, columns), lambda h: (0, h, 0, 0))
    return pl.pallas_call(
        lambda *refs: place_body(side, *refs),
        out_shape=jax.ShapeDtypeStruct((side * rows, model), jnp.float32),
        grid=(halves,),
        in_specs=[pl.BlockSpec(memory_space=pltpu.SMEM)] + [block] * (2 * side),
        out_specs=pl.BlockSpec((side * rows, model // halves), lambda h: (0, h)),
        compiler_params=params(),
        cost_estimate=NO_COST,
        name="place_blocks",
    )(spot, *first, *second)


def at(array, index, axis=0):
    return lax.dynamic_index_in_dim(array, index, axis, keepdims=False)


def on_device(head_output, router_logits, chosen_slots, block_owner, out_weight, cotangent):
    n_dp, n_fsdp = lax.axis_size("dp"), lax.axis_size("fsdp")
    dp, fsdp = lax.axis_index("dp"), lax.axis_index("fsdp")
    side, chips = math.isqrt(n_dp), n_fsdp // 2
    y, z = dp // side, dp % side
    chip, core = fsdp // 2, fsdp % 2

    def along_x(value, ahead):
        return lax.ppermute(value, "fsdp", [(f, (f + 2 * ahead) % n_fsdp) for f in range(n_fsdp)])

    def along_y(value, ahead):
        return lax.ppermute(value, "dp", [(d, (d + side * ahead) % n_dp) for d in range(n_dp)])

    def along_z(value, ahead):
        return lax.ppermute(
            value, "dp", [(d, d // side * side + (d + ahead) % side) for d in range(n_dp)]
        )

    def to_partner(value):
        return lax.ppermute(value, "fsdp", [(f, f ^ 1) for f in range(n_fsdp)])

    slots = chosen_slots.shape[1]
    blocks = block_owner.shape[1]
    block = slots // blocks
    tokens, width = head_output.shape
    shard, model = out_weight.shape
    rows = cotangent.shape[0]
    receive = rows // block
    scale = 1.0 / math.sqrt(rows * n_dp * n_fsdp)
    half = model // 2
    owner = block_owner[0]

    weight = lax.all_gather(out_weight, "fsdp", axis=0, tiled=True)

    own_cot = lax.dynamic_slice(cotangent, (0, core * half), (rows, half))
    partner_cot = to_partner(lax.dynamic_slice(cotangent, (0, (1 - core) * half), (rows, half)))

    peers = jnp.arange(n_dp, dtype=jnp.int32)
    match = owner[None, :] == peers[:, None]
    send = pick_rows(owner, chosen_slots.reshape(slots, 1), router_logits.reshape(1, tokens), head_output)
    send = send.reshape(n_dp, block, width + EXTRA)
    got = lax.all_to_all(send, "dp", split_axis=0, concat_axis=0, tiled=True)

    got = after(got, partner_cot)
    incoming = (got[:, 0, width + 1] > 0.5).astype(jnp.int32)
    position = jnp.cumsum(incoming) - 1
    ids = jnp.arange(receive, dtype=jnp.int32)
    source = jnp.sum(
        jnp.where((position[None, :] == ids[:, None]) & (incoming[None, :] > 0), peers[None, :], 0),
        axis=1,
    )
    held = move_blocks(got, source, width + EXTRA).reshape(rows, width + EXTRA)

    both = jnp.concatenate([held, to_partner(held)], axis=0)
    both_cot = jnp.concatenate([own_cot, partner_cot], axis=0)
    gate = both[:, width].astype(jnp.float32)
    weighted = (gate[:, None] * both_cot.astype(jnp.float32)).astype(jnp.bfloat16)
    both_rows = both[:, :width]
    part = half // (2 * side)
    cut = width // 2

    def term(first, index):
        columns = lax.dynamic_slice(weighted, (0, first + index % side * part), (2 * rows, part))
        product = lax.dot_general(
            both_rows, columns, (((0,), (0,)), ((), ())), preferred_element_type=jnp.float32
        )
        return product * scale

    def wide(value):
        return value.astype(jnp.float32)

    def narrow(value):
        return value.astype(jnp.bfloat16)

    far_y, far_z = narrow(term(0, y + 2)), narrow(term(half // 2, z + 2))
    got_parts = (
        along_y(far_y[:cut], 1), along_z(far_z[:cut], 1), along_y(far_y[cut:], -1), along_z(far_z[cut:], -1)
    )
    ahead_y, ahead_z = term(0, y + 1), term(half // 2, z + 1)
    behind_y, behind_z = term(0, y + side - 1), term(half // 2, z + side - 1)
    got_parts = after(got_parts, ahead_y, ahead_z, behind_y, behind_z)
    low_y, low_z, high_y, high_z = [wide(part_sum) for part_sum in got_parts]
    sent = (
        narrow(jnp.concatenate([ahead_y[:cut] + low_y, ahead_y[cut:]], axis=0)),
        narrow(jnp.concatenate([ahead_z[:cut] + low_z, ahead_z[cut:]], axis=0)),
        narrow(jnp.concatenate([behind_y[:cut], behind_y[cut:] + high_y], axis=0)),
        narrow(jnp.concatenate([behind_z[:cut], behind_z[cut:] + high_z], axis=0)),
    )
    from_y, from_z = along_y(sent[0], 1), along_z(sent[1], 1)
    to_y, to_z = along_y(sent[2], -1), along_z(sent[3], -1)

    slot = after(jnp.clip(position, 0, receive - 1), sent)
    update, back = project(held, weight, cotangent, slot, block)
    returned = lax.all_to_all(back, "dp", split_axis=0, concat_axis=0, tiled=True)
    from_y, to_y, from_z, to_z = after((from_y, to_y, from_z, to_z), back)

    sum_y = narrow(term(0, y) + wide(from_y) + wide(to_y))
    sum_z = narrow(term(half // 2, z) + wide(from_z) + wide(to_z))

    share = shard // side

    def exchange(value, axis, place, along):
        count = value.shape[axis]
        total = wide(at(value, place, axis))
        for ahead in range(1, count):
            total += wide(along(at(value, (place + ahead) % count, axis), ahead))
        return narrow(total)

    sum_y = exchange(sum_y.reshape(n_fsdp, side, share, part), 1, z, along_z)
    sum_z = exchange(sum_z.reshape(n_fsdp, side, share, part), 1, y, along_y)
    sums = jnp.stack([sum_y, sum_z]).reshape(2, chips, 2, share, part)
    sums = exchange(after(sums, returned), 1, chip, along_x)
    keep, take = at(sums, core, 1), to_partner(at(sums, 1 - core, 1))
    first = core == 0
    piece = jnp.stack([jnp.where(first, keep, take), jnp.where(first, take, keep)])

    def around(value, along):
        return [value] + [along(value, ahead) for ahead in range(1, side)]

    line_z = jnp.stack(around(piece[:, 0], along_z))
    line_y = jnp.stack(around(piece[:, 1], along_y))
    spot = jnp.stack([y, z]).astype(jnp.int32)
    grad_weight = place_blocks(spot, around(line_z, along_y), around(line_y, along_z))

    grad_context = move_blocks(returned, owner, width).reshape(slots, width)
    logit_blocks = returned[:, :, width]
    grad_logit = jnp.sum(jnp.where(match[:, :, None], logit_blocks[:, None, :], 0), axis=0).reshape(-1)
    return (update, grad_context, narrow(grad_logit), grad_weight)


def solution(mesh):
    placed = (
        P(("dp", "fsdp"), None),
        P(("dp", "fsdp")),
        P(("dp", "fsdp"), None),
        P(("dp", "fsdp"), None),
        P("fsdp", None),
        P(("dp", "fsdp"), None),
    )
    return jax.shard_map(
        on_device,
        mesh=mesh,
        in_specs=placed,
        out_specs=(
            P(("dp", "fsdp"), None),
            P(("dp", "fsdp"), None),
            P(("dp", "fsdp")),
            P("fsdp", None),
        ),
        check_vma=False,
    )
```

```python
import math

import jax
import jax.numpy as jnp
from jax import lax
from jax.experimental import pallas as pl
from jax.experimental.pallas import tpu as pltpu
from jax.sharding import PartitionSpec as P

EXTRA = 128
MIB = 1024 * 1024
NO_COST = pl.CostEstimate(flops=0, bytes_accessed=0, transcendentals=0)


def params(limit=24):
    return pltpu.CompilerParams(vmem_limit_bytes=limit * MIB)


def after(value, *others):
    return lax.optimization_barrier((value, others))[0]


def pick_body(owner_ref, listed_ref, logit_ref, head_ref, out_ref, onehot_ref, head, picked, in_sems, out_sems):
    rows, count = onehot_ref.shape
    blocks = owner_ref.shape[0]
    block = rows // blocks
    steps = in_sems.shape[0]
    width = head.shape[1]
    columns = width // steps

    def fetch(step):
        span = pl.ds(step * columns, columns)
        return pltpu.make_async_copy(head_ref.at[:, span], head.at[:, span], in_sems.at[step])

    def hand_over(step):
        span = pl.ds(step * columns, columns if step < steps else EXTRA)
        return pltpu.make_async_copy(picked.at[:, span], out_ref.at[:, span], out_sems.at[step])

    for step in range(steps):
        fetch(step).start()

    lane = lax.broadcasted_iota(jnp.int32, (block, EXTRA), 1)
    tokens = lax.broadcasted_iota(jnp.int32, (block, count), 1)
    for peer in range(rows // block):
        found = jnp.int32(blocks)
        for b in range(blocks):
            found = jnp.where(owner_ref[b] == peer, b, found)
        there = found < blocks
        start = pl.multiple_of(jnp.minimum(found, blocks - 1) * block, block)
        listed = jnp.where(there, listed_ref[pl.ds(start, block), :], -1)
        hit = listed == tokens
        span = slice(peer * block, (peer + 1) * block)
        onehot_ref[span, :] = hit.astype(jnp.bfloat16)
        logit = jnp.sum(jnp.where(hit, logit_ref[...], 0.0), axis=1, keepdims=True)
        mark = jnp.where(there, 1.0, 0.0)
        picked[span, width:] = jnp.where(lane == 0, jax.nn.sigmoid(logit), mark).astype(jnp.bfloat16)
    hand_over(steps).start()

    for step in range(steps):
        fetch(step).wait()
        span = slice(step * columns, (step + 1) * columns)
        picked[:, span] = jnp.dot(
            onehot_ref[...], head[:, span], preferred_element_type=jnp.float32
        ).astype(jnp.bfloat16)
        hand_over(step).start()
    for step in range(steps + 1):
        hand_over(step).wait()


def pick_rows(owner, listed, logits, head):
    rows = listed.shape[0]
    count, width = head.shape
    steps = width // 512
    vmem = pl.BlockSpec(memory_space=pltpu.VMEM)
    return pl.pallas_call(
        pick_body,
        out_shape=jax.ShapeDtypeStruct((rows, width + EXTRA), jnp.bfloat16),
        in_specs=[
            pl.BlockSpec(memory_space=pltpu.SMEM),
            vmem,
            vmem,
            pl.BlockSpec(memory_space=pl.ANY),
        ],
        out_specs=pl.BlockSpec(memory_space=pl.ANY),
        scratch_shapes=[
            pltpu.VMEM((rows, count), jnp.bfloat16),
            pltpu.VMEM((count, width), jnp.bfloat16),
            pltpu.VMEM((rows, width + EXTRA), jnp.bfloat16),
            pltpu.SemaphoreType.DMA((steps,)),
            pltpu.SemaphoreType.DMA((steps + 1,)),
        ],
        compiler_params=params(56),
        cost_estimate=NO_COST,
        name="pick_rows",
    )(owner, listed, logits, head)


def move_body(width, index_ref, source_ref, out_ref):
    blocks = source_ref.shape[0]
    for slot in range(out_ref.shape[0]):
        block = index_ref[slot]

        @pl.when(block < blocks)
        def _():
            out_ref[slot] = source_ref[jnp.minimum(block, blocks - 1), :, :width]

        @pl.when(block >= blocks)
        def _():
            out_ref[slot] = jnp.zeros(out_ref.shape[1:], out_ref.dtype)


def move_blocks(source, index, width):
    blocks, rows, _ = source.shape
    copies = index.shape[0]
    return pl.pallas_call(
        lambda *refs: move_body(width, *refs),
        out_shape=jax.ShapeDtypeStruct((copies, rows, width), source.dtype),
        in_specs=[
            pl.BlockSpec(memory_space=pltpu.SMEM),
            pl.BlockSpec(memory_space=pltpu.VMEM),
        ],
        out_specs=pl.BlockSpec(memory_space=pltpu.VMEM),
        compiler_params=params(),
        cost_estimate=NO_COST,
        name="move_blocks",
    )(index, source)


def answer_body(width, slot_ref, rows_ref, weight_ref, cot_ref, back_ref, total_ref, logit_ref):
    step = pl.program_id(0)

    @pl.when(step == 0)
    def _():
        total_ref[...] = jnp.zeros_like(total_ref)

    total_ref[...] += lax.dot_general(
        cot_ref[...], weight_ref[...], (((1,), (1,)), ((), ())), preferred_element_type=jnp.float32
    )

    @pl.when(step == pl.num_programs(0) - 1)
    def _():
        gate = rows_ref[:, width : width + 1].astype(jnp.float32)
        inner = jnp.sum(rows_ref[:, :width].astype(jnp.float32) * total_ref[...], axis=1, keepdims=True)
        logit_ref[...] = jnp.broadcast_to(gate * (1.0 - gate) * inner, logit_ref.shape)
        total_ref[...] *= gate
        block = back_ref.shape[1]
        for peer in range(back_ref.shape[0]):
            here = pl.ds(pl.multiple_of(slot_ref[peer] * block, block), block)
            back_ref[peer, :, :width] = total_ref[here, :].astype(jnp.bfloat16)
            back_ref[peer, :, width:] = logit_ref[here, :].astype(jnp.bfloat16)


def answer(rows, weight, cotangent, slots, block):
    count, wide = rows.shape
    width, model = weight.shape
    columns = 1024
    return pl.pallas_call(
        lambda *refs: answer_body(width, *refs),
        out_shape=jax.ShapeDtypeStruct((slots.shape[0], block, wide), jnp.bfloat16),
        grid=(model // columns,),
        in_specs=[
            pl.BlockSpec(memory_space=pltpu.SMEM),
            pl.BlockSpec((count, wide), lambda n: (0, 0)),
            pl.BlockSpec((width, columns), lambda n: (0, n)),
            pl.BlockSpec((count, columns), lambda n: (0, n)),
        ],
        out_specs=pl.BlockSpec((slots.shape[0], block, wide), lambda n: (0, 0, 0)),
        scratch_shapes=[
            pltpu.VMEM((count, width), jnp.float32),
            pltpu.VMEM((count, EXTRA), jnp.float32),
        ],
        compiler_params=params(56),
        cost_estimate=NO_COST,
        name="answer",
    )(slots, rows, weight, cotangent)


def project_body(width, rows_ref, weight_ref, update_ref):
    gate = rows_ref[:, width : width + 1].astype(jnp.float32)
    projected = jnp.dot(rows_ref[:, :width], weight_ref[...], preferred_element_type=jnp.float32)
    update_ref[...] = (gate * projected).astype(jnp.bfloat16)


def project(rows, weight):
    count, wide = rows.shape
    width, model = weight.shape
    columns = 1024
    return pl.pallas_call(
        lambda *refs: project_body(width, *refs),
        out_shape=jax.ShapeDtypeStruct((count, model), jnp.bfloat16),
        grid=(model // columns,),
        in_specs=[
            pl.BlockSpec((count, wide), lambda n: (0, 0)),
            pl.BlockSpec((width, columns), lambda n: (0, n)),
        ],
        out_specs=pl.BlockSpec((count, columns), lambda n: (0, n)),
        compiler_params=params(56),
        cost_estimate=NO_COST,
        name="project",
    )(rows, weight)


def place_body(side, spot_ref, *refs):
    out_ref = refs[-1]
    columns = refs[0].shape[2]
    for which in range(2):
        for ahead in range(side):
            left = (spot_ref[which] - ahead + side) % side * columns + which * side * columns
            array = refs[which * side + ahead]
            out_ref[:, pl.ds(pl.multiple_of(left, columns), columns)] = array[0].astype(jnp.float32)


def place_blocks(spot, first, second):
    side = len(first)
    halves, rows, columns = first[0].shape
    model = halves * 2 * side * columns
    block = pl.BlockSpec((1, rows, columns), lambda h: (h, 0, 0))
    return pl.pallas_call(
        lambda *refs: place_body(side, *refs),
        out_shape=jax.ShapeDtypeStruct((rows, model), jnp.float32),
        grid=(halves,),
        in_specs=[pl.BlockSpec(memory_space=pltpu.SMEM)] + [block] * (2 * side),
        out_specs=pl.BlockSpec((rows, model // halves), lambda h: (0, h)),
        compiler_params=params(),
        cost_estimate=NO_COST,
        name="place_blocks",
    )(spot, *first, *second)


def at(array, index, axis=0):
    return lax.dynamic_index_in_dim(array, index, axis, keepdims=False)


def on_device(head_output, router_logits, chosen_slots, block_owner, out_weight, cotangent):
    n_dp, n_fsdp = lax.axis_size("dp"), lax.axis_size("fsdp")
    dp, fsdp = lax.axis_index("dp"), lax.axis_index("fsdp")
    side, chips = math.isqrt(n_dp), n_fsdp // 2
    y, z = dp // side, dp % side
    chip, core = fsdp // 2, fsdp % 2

    def along_x(value, ahead):
        return lax.ppermute(value, "fsdp", [(f, (f + 2 * ahead) % n_fsdp) for f in range(n_fsdp)])

    def along_y(value, ahead):
        return lax.ppermute(value, "dp", [(d, (d + side * ahead) % n_dp) for d in range(n_dp)])

    def along_z(value, ahead):
        return lax.ppermute(
            value, "dp", [(d, d // side * side + (d + ahead) % side) for d in range(n_dp)]
        )

    def to_partner(value):
        return lax.ppermute(value, "fsdp", [(f, f ^ 1) for f in range(n_fsdp)])

    slots = chosen_slots.shape[1]
    blocks = block_owner.shape[1]
    block = slots // blocks
    tokens, width = head_output.shape
    shard, model = out_weight.shape
    rows = cotangent.shape[0]
    receive = rows // block
    scale = 1.0 / math.sqrt(rows * n_dp * n_fsdp)
    half = model // 2
    owner = block_owner[0]

    weight = lax.all_gather(out_weight, "fsdp", axis=0, tiled=True)

    own_cot = lax.dynamic_slice(cotangent, (0, core * half), (rows, half))
    partner_cot = to_partner(lax.dynamic_slice(cotangent, (0, (1 - core) * half), (rows, half)))

    peers = jnp.arange(n_dp, dtype=jnp.int32)
    match = owner[None, :] == peers[:, None]
    send = pick_rows(owner, chosen_slots.reshape(slots, 1), router_logits.reshape(1, tokens), head_output)
    send = send.reshape(n_dp, block, width + EXTRA)
    got = lax.all_to_all(send, "dp", split_axis=0, concat_axis=0, tiled=True)

    got = after(got, partner_cot)
    incoming = (got[:, 0, width + 1] > 0.5).astype(jnp.int32)
    position = jnp.cumsum(incoming) - 1
    ids = jnp.arange(receive, dtype=jnp.int32)
    source = jnp.sum(
        jnp.where((position[None, :] == ids[:, None]) & (incoming[None, :] > 0), peers[None, :], 0),
        axis=1,
    )
    held = move_blocks(got, source, width + EXTRA).reshape(rows, width + EXTRA)

    both = jnp.concatenate([held, to_partner(held)], axis=0)
    both_cot = jnp.concatenate([own_cot, partner_cot], axis=0)
    gate = both[:, width].astype(jnp.float32)
    weighted = (gate[:, None] * both_cot.astype(jnp.float32)).astype(jnp.bfloat16)
    both_rows = both[:, :width]
    part = half // (2 * side)
    cut = width // 2

    def term(first, index):
        columns = lax.dynamic_slice(weighted, (0, first + index % side * part), (2 * rows, part))
        product = lax.dot_general(
            both_rows, columns, (((0,), (0,)), ((), ())), preferred_element_type=jnp.float32
        )
        return product * scale

    def wide(value):
        return value.astype(jnp.float32)

    def narrow(value):
        return value.astype(jnp.bfloat16)

    far_y, far_z = narrow(term(0, y + 2)), narrow(term(half // 2, z + 2))
    got_parts = (
        along_y(far_y[:cut], 1), along_z(far_z[:cut], 1), along_y(far_y[cut:], -1), along_z(far_z[cut:], -1)
    )
    ahead_y, ahead_z = term(0, y + 1), term(half // 2, z + 1)
    behind_y, behind_z = term(0, y + side - 1), term(half // 2, z + side - 1)
    own_y, own_z = term(0, y), term(half // 2, z)
    got_parts = after(got_parts, ahead_y, ahead_z, behind_y, behind_z, own_y, own_z)
    low_y, low_z, high_y, high_z = [wide(part_sum) for part_sum in got_parts]
    sent = (
        narrow(jnp.concatenate([ahead_y[:cut] + low_y, ahead_y[cut:]], axis=0)),
        narrow(jnp.concatenate([ahead_z[:cut] + low_z, ahead_z[cut:]], axis=0)),
        narrow(jnp.concatenate([behind_y[:cut], behind_y[cut:] + high_y], axis=0)),
        narrow(jnp.concatenate([behind_z[:cut], behind_z[cut:] + high_z], axis=0)),
    )
    from_y, from_z = along_y(sent[0], 1), along_z(sent[1], 1)
    to_y, to_z = along_y(sent[2], -1), along_z(sent[3], -1)

    slot = after(jnp.clip(position, 0, receive - 1), sent)
    back = answer(held, weight, cotangent, slot, block)
    returned = lax.all_to_all(back, "dp", split_axis=0, concat_axis=0, tiled=True)
    from_y, to_y, from_z, to_z = after((from_y, to_y, from_z, to_z), back)

    sum_y = narrow(own_y + wide(from_y) + wide(to_y))
    sum_z = narrow(own_z + wide(from_z) + wide(to_z))

    share = shard // side

    def exchange(value, axis, place, along):
        count = value.shape[axis]
        total = wide(at(value, place, axis))
        for ahead in range(1, count):
            total += wide(along(at(value, (place + ahead) % count, axis), ahead))
        return narrow(total)

    sums = jnp.stack([sum_y, sum_z]).reshape(2, chips, 2 * shard, part)
    update = project(after(held, sums), weight)
    sums = exchange(sums, 1, chip, along_x)
    sums = after(sums, returned, update).reshape(2, 2, shard, part)
    keep, take = at(sums, core, 1), to_partner(at(sums, 1 - core, 1))
    first = core == 0
    piece = jnp.stack([jnp.where(first, keep, take), jnp.where(first, take, keep)], axis=1)

    def around(value, along):
        return [value] + [along(value, ahead) for ahead in range(1, side)]

    def whole(value, along):
        terms = [wide(term) for term in around(value, along)]
        return narrow((terms[0] + terms[2]) + (terms[1] + terms[3]))

    sum_y, sum_z = whole(piece[0], along_z), whole(piece[1], along_y)
    spot = jnp.stack([y, z]).astype(jnp.int32)
    grad_weight = place_blocks(spot, around(sum_y, along_y), around(sum_z, along_z))

    grad_context = move_blocks(returned, owner, width).reshape(slots, width)
    logit_blocks = returned[:, :, width]
    grad_logit = jnp.sum(jnp.where(match[:, :, None], logit_blocks[:, None, :], 0), axis=0).reshape(-1)
    return (update, grad_context, narrow(grad_logit), grad_weight)


def solution(mesh):
    placed = (
        P(("dp", "fsdp"), None),
        P(("dp", "fsdp")),
        P(("dp", "fsdp"), None),
        P(("dp", "fsdp"), None),
        P("fsdp", None),
        P(("dp", "fsdp"), None),
    )
    return jax.shard_map(
        on_device,
        mesh=mesh,
        in_specs=placed,
        out_specs=(
            P(("dp", "fsdp"), None),
            P(("dp", "fsdp"), None),
            P(("dp", "fsdp")),
            P("fsdp", None),
        ),
        check_vma=False,
    )
```

```python
import math

import jax
import jax.numpy as jnp
from jax import lax
from jax.experimental import pallas as pl
from jax.experimental.pallas import tpu as pltpu
from jax.sharding import PartitionSpec as P

EXTRA = 128
MIB = 1024 * 1024
NO_COST = pl.CostEstimate(flops=0, bytes_accessed=0, transcendentals=0)


def params(limit=24):
    return pltpu.CompilerParams(vmem_limit_bytes=limit * MIB)


def after(value, *others):
    return lax.optimization_barrier((value, others))[0]


def pick_body(owner_ref, listed_ref, logit_ref, head_ref, out_ref, onehot_ref, head, picked, in_sems, out_sems):
    rows, count = onehot_ref.shape
    blocks = owner_ref.shape[0]
    block = rows // blocks
    steps = in_sems.shape[0]
    width = head.shape[1]
    columns = width // steps

    def fetch(step):
        span = pl.ds(step * columns, columns)
        return pltpu.make_async_copy(head_ref.at[:, span], head.at[:, span], in_sems.at[step])

    def hand_over(step):
        span = pl.ds(step * columns, columns if step < steps else EXTRA)
        return pltpu.make_async_copy(picked.at[:, span], out_ref.at[:, span], out_sems.at[step])

    for step in range(steps):
        fetch(step).start()

    tokens = lax.broadcasted_iota(jnp.int32, (block, count), 1)
    for peer in range(rows // block):
        found = jnp.int32(blocks)
        for b in range(blocks):
            found = jnp.where(owner_ref[b] == peer, b, found)
        start = pl.multiple_of(jnp.minimum(found, blocks - 1) * block, block)
        listed = jnp.where(found < blocks, listed_ref[pl.ds(start, block), :], -1)
        onehot_ref[peer * block : (peer + 1) * block, :] = (listed == tokens).astype(jnp.bfloat16)
    first = lax.broadcasted_iota(jnp.int32, (EXTRA, count), 0) == 0
    extra = jnp.where(first, jax.nn.sigmoid(logit_ref[...]), 1.0).astype(jnp.bfloat16)
    picked[:, width:] = lax.dot_general(
        onehot_ref[...], extra, (((1,), (1,)), ((), ())), preferred_element_type=jnp.float32
    ).astype(jnp.bfloat16)
    hand_over(steps).start()

    for step in range(steps):
        fetch(step).wait()
        span = slice(step * columns, (step + 1) * columns)
        picked[:, span] = jnp.dot(
            onehot_ref[...], head[:, span], preferred_element_type=jnp.float32
        ).astype(jnp.bfloat16)
        hand_over(step).start()
    for step in range(steps + 1):
        hand_over(step).wait()


def pick_rows(owner, listed, logits, head):
    rows = listed.shape[0]
    count, width = head.shape
    steps = width // 512
    vmem = pl.BlockSpec(memory_space=pltpu.VMEM)
    return pl.pallas_call(
        pick_body,
        out_shape=jax.ShapeDtypeStruct((rows, width + EXTRA), jnp.bfloat16),
        in_specs=[
            pl.BlockSpec(memory_space=pltpu.SMEM),
            vmem,
            vmem,
            pl.BlockSpec(memory_space=pl.ANY),
        ],
        out_specs=pl.BlockSpec(memory_space=pl.ANY),
        scratch_shapes=[
            pltpu.VMEM((rows, count), jnp.bfloat16),
            pltpu.VMEM((count, width), jnp.bfloat16),
            pltpu.VMEM((rows, width + EXTRA), jnp.bfloat16),
            pltpu.SemaphoreType.DMA((steps,)),
            pltpu.SemaphoreType.DMA((steps + 1,)),
        ],
        compiler_params=params(56),
        cost_estimate=NO_COST,
        name="pick_rows",
    )(owner, listed, logits, head)


def move_body(width, index_ref, source_ref, out_ref):
    blocks = source_ref.shape[0]
    for slot in range(out_ref.shape[0]):
        block = index_ref[slot]

        @pl.when(block < blocks)
        def _():
            out_ref[slot] = source_ref[jnp.minimum(block, blocks - 1), :, :width]

        @pl.when(block >= blocks)
        def _():
            out_ref[slot] = jnp.zeros(out_ref.shape[1:], out_ref.dtype)


def move_blocks(source, index, width):
    blocks, rows, _ = source.shape
    copies = index.shape[0]
    return pl.pallas_call(
        lambda *refs: move_body(width, *refs),
        out_shape=jax.ShapeDtypeStruct((copies, rows, width), source.dtype),
        in_specs=[
            pl.BlockSpec(memory_space=pltpu.SMEM),
            pl.BlockSpec(memory_space=pltpu.VMEM),
        ],
        out_specs=pl.BlockSpec(memory_space=pltpu.VMEM),
        compiler_params=params(),
        cost_estimate=NO_COST,
        name="move_blocks",
    )(index, source)


def answer_body(width, slot_ref, rows_ref, weight_ref, cot_ref, back_ref, total_ref, logit_ref):
    step = pl.program_id(0)

    @pl.when(step == 0)
    def _():
        total_ref[...] = jnp.zeros_like(total_ref)

    total_ref[...] += lax.dot_general(
        cot_ref[...], weight_ref[...], (((1,), (1,)), ((), ())), preferred_element_type=jnp.float32
    )

    @pl.when(step == pl.num_programs(0) - 1)
    def _():
        gate = rows_ref[:, width : width + 1].astype(jnp.float32)
        inner = jnp.sum(rows_ref[:, :width].astype(jnp.float32) * total_ref[...], axis=1, keepdims=True)
        logit_ref[...] = jnp.broadcast_to(gate * (1.0 - gate) * inner, logit_ref.shape)
        total_ref[...] *= gate
        block = back_ref.shape[1]
        for peer in range(back_ref.shape[0]):
            here = pl.ds(pl.multiple_of(slot_ref[peer] * block, block), block)
            back_ref[peer, :, :width] = total_ref[here, :].astype(jnp.bfloat16)
            back_ref[peer, :, width:] = logit_ref[here, :].astype(jnp.bfloat16)


def answer(rows, weight, cotangent, slots, block):
    count, wide = rows.shape
    width, model = weight.shape
    columns = 1024
    return pl.pallas_call(
        lambda *refs: answer_body(width, *refs),
        out_shape=jax.ShapeDtypeStruct((slots.shape[0], block, wide), jnp.bfloat16),
        grid=(model // columns,),
        in_specs=[
            pl.BlockSpec(memory_space=pltpu.SMEM),
            pl.BlockSpec((count, wide), lambda n: (0, 0)),
            pl.BlockSpec((width, columns), lambda n: (0, n)),
            pl.BlockSpec((count, columns), lambda n: (0, n)),
        ],
        out_specs=pl.BlockSpec((slots.shape[0], block, wide), lambda n: (0, 0, 0)),
        scratch_shapes=[
            pltpu.VMEM((count, width), jnp.float32),
            pltpu.VMEM((count, EXTRA), jnp.float32),
        ],
        compiler_params=params(56),
        cost_estimate=NO_COST,
        name="answer",
    )(slots, rows, weight, cotangent)


def project_body(width, rows_ref, weight_ref, update_ref):
    gate = rows_ref[:, width : width + 1].astype(jnp.float32)
    projected = jnp.dot(rows_ref[:, :width], weight_ref[...], preferred_element_type=jnp.float32)
    update_ref[...] = (gate * projected).astype(jnp.bfloat16)


def project(rows, weight):
    count, wide = rows.shape
    width, model = weight.shape
    columns = 1024
    return pl.pallas_call(
        lambda *refs: project_body(width, *refs),
        out_shape=jax.ShapeDtypeStruct((count, model), jnp.bfloat16),
        grid=(model // columns,),
        in_specs=[
            pl.BlockSpec((count, wide), lambda n: (0, 0)),
            pl.BlockSpec((width, columns), lambda n: (0, n)),
        ],
        out_specs=pl.BlockSpec((count, columns), lambda n: (0, n)),
        compiler_params=params(56),
        cost_estimate=NO_COST,
        name="project",
    )(rows, weight)


def place_body(side, spot_ref, *refs):
    out_ref = refs[-1]
    columns = refs[0].shape[2]
    for which in range(2):
        for ahead in range(side):
            left = (spot_ref[which] - ahead + side) % side * columns + which * side * columns
            array = refs[which * side + ahead]
            out_ref[:, pl.ds(pl.multiple_of(left, columns), columns)] = array[0].astype(jnp.float32)


def place_blocks(spot, first, second):
    side = len(first)
    halves, rows, columns = first[0].shape
    model = halves * 2 * side * columns
    block = pl.BlockSpec((1, rows, columns), lambda h, spot_ref: (h, 0, 0))
    return pl.pallas_call(
        lambda *refs: place_body(side, *refs),
        out_shape=jax.ShapeDtypeStruct((rows, model), jnp.float32),
        grid_spec=pltpu.PrefetchScalarGridSpec(
            num_scalar_prefetch=1,
            grid=(halves,),
            in_specs=[block] * (2 * side),
            out_specs=pl.BlockSpec((rows, model // halves), lambda h, spot_ref: (0, (h + spot_ref[2]) % halves)),
        ),
        compiler_params=params(),
        cost_estimate=NO_COST,
        name="place_blocks",
    )(spot, *first, *second)


def at(array, index, axis=0):
    return lax.dynamic_index_in_dim(array, index, axis, keepdims=False)


def on_device(head_output, router_logits, chosen_slots, block_owner, out_weight, cotangent):
    n_dp, n_fsdp = lax.axis_size("dp"), lax.axis_size("fsdp")
    dp, fsdp = lax.axis_index("dp"), lax.axis_index("fsdp")
    side, chips = math.isqrt(n_dp), n_fsdp // 2
    y, z = dp // side, dp % side
    chip, core = fsdp // 2, fsdp % 2

    def along_x(value, ahead):
        return lax.ppermute(value, "fsdp", [(f, (f + 2 * ahead) % n_fsdp) for f in range(n_fsdp)])

    def along_y(value, ahead):
        return lax.ppermute(value, "dp", [(d, (d + side * ahead) % n_dp) for d in range(n_dp)])

    def along_z(value, ahead):
        return lax.ppermute(
            value, "dp", [(d, d // side * side + (d + ahead) % side) for d in range(n_dp)]
        )

    def to_partner(value):
        return lax.ppermute(value, "fsdp", [(f, f ^ 1) for f in range(n_fsdp)])

    slots = chosen_slots.shape[1]
    blocks = block_owner.shape[1]
    block = slots // blocks
    tokens, width = head_output.shape
    shard, model = out_weight.shape
    rows = cotangent.shape[0]
    receive = rows // block
    scale = 1.0 / math.sqrt(rows * n_dp * n_fsdp)
    half = model // 2
    owner = block_owner[0]

    weight = lax.all_gather(out_weight, "fsdp", axis=0, tiled=True)

    own_cot = lax.dynamic_slice(cotangent, (0, core * half), (rows, half))
    partner_cot = to_partner(lax.dynamic_slice(cotangent, (0, (1 - core) * half), (rows, half)))

    peers = jnp.arange(n_dp, dtype=jnp.int32)
    match = owner[None, :] == peers[:, None]
    send = pick_rows(owner, chosen_slots.reshape(slots, 1), router_logits.reshape(1, tokens), head_output)
    send = send.reshape(n_dp, block, width + EXTRA)
    got = lax.all_to_all(send, "dp", split_axis=0, concat_axis=0, tiled=True)

    got = after(got, partner_cot)
    incoming = (got[:, 0, width + 1] > 0.5).astype(jnp.int32)
    position = jnp.cumsum(incoming) - 1
    ids = jnp.arange(receive, dtype=jnp.int32)
    source = jnp.sum(
        jnp.where((position[None, :] == ids[:, None]) & (incoming[None, :] > 0), peers[None, :], 0),
        axis=1,
    )
    held = move_blocks(got, source, width + EXTRA).reshape(rows, width + EXTRA)

    both = jnp.concatenate([held, to_partner(held)], axis=0)
    both_cot = jnp.concatenate([own_cot, partner_cot], axis=0)
    gate = both[:, width].astype(jnp.float32)
    weighted = (gate[:, None] * both_cot.astype(jnp.float32)).astype(jnp.bfloat16)
    both_rows = both[:, :width]
    part = half // (2 * side)

    def term(first, index):
        columns = lax.dynamic_slice(weighted, (0, first + index % side * part), (2 * rows, part))
        product = lax.dot_general(
            both_rows, columns, (((0,), (0,)), ((), ())), preferred_element_type=jnp.float32
        )
        return product * scale

    def wide(value):
        return value.astype(jnp.float32)

    def narrow(value):
        return value.astype(jnp.bfloat16)

    cut = width // 2
    far_y, far_z = narrow(term(0, y + 2)), narrow(term(half // 2, z + 2))
    got_parts = (
        along_y(far_y[:cut], 1), along_z(far_z[:cut], 1), along_y(far_y[cut:], -1), along_z(far_z[cut:], -1)
    )
    ahead_y, ahead_z = term(0, y + 1), term(half // 2, z + 1)
    behind_y, behind_z = term(0, y + side - 1), term(half // 2, z + side - 1)
    own_y, own_z = narrow(term(0, y)), narrow(term(half // 2, z))
    got_parts = after(got_parts, ahead_y, ahead_z, behind_y, behind_z, own_y, own_z)
    low_y, low_z, high_y, high_z = [wide(part_sum) for part_sum in got_parts]
    sent = (
        narrow(jnp.concatenate([ahead_y[:cut] + low_y, ahead_y[cut:]], axis=0)),
        narrow(jnp.concatenate([ahead_z[:cut] + low_z, ahead_z[cut:]], axis=0)),
        narrow(jnp.concatenate([behind_y[:cut], behind_y[cut:] + high_y], axis=0)),
        narrow(jnp.concatenate([behind_z[:cut], behind_z[cut:] + high_z], axis=0)),
    )
    from_y, from_z = along_y(sent[0], 1), along_z(sent[1], 1)
    to_y, to_z = along_y(sent[2], -1), along_z(sent[3], -1)

    slot = after(jnp.clip(position, 0, receive - 1), sent)
    back = answer(held, weight, cotangent, slot, block)
    returned = lax.all_to_all(back, "dp", split_axis=0, concat_axis=0, tiled=True)
    from_y, to_y, from_z, to_z = after((from_y, to_y, from_z, to_z), back)

    def rows_of(ahead):
        start = (chip + ahead) % chips * (2 * shard)

        def cut_out(value):
            return wide(lax.dynamic_slice(value, (start, 0), (2 * shard, part)))

        return jnp.stack(
            [
                cut_out(own) + cut_out(up) + cut_out(down)
                for own, up, down in ((own_y, from_y, to_y), (own_z, from_z, to_z))
            ]
        )

    order = [2, 1] + list(range(3, chips))
    chunks = [narrow(rows_of(ahead)) for ahead in order]
    terms = [rows_of(0)] + [along_x(chunk, ahead) for chunk, ahead in zip(chunks, order)]
    update = project(after(held, *chunks), weight)
    terms = after(terms, returned, update)

    def rows_for(which):
        total = sum(wide(at(term_x.reshape(2, 2, shard, part), which, 1)) for term_x in terms)
        return narrow(total)

    take = to_partner(rows_for(1 - core))
    keep = rows_for(core)

    def around(value, along):
        return [value] + [along(value, ahead) for ahead in range(1, side)]

    def whole(value, along):
        values = [wide(one) for one in around(value, along)]
        return narrow((values[0] + values[2]) + (values[1] + values[3]))

    sum_y = whole(jnp.stack([keep[0], take[0]]), along_z)
    sum_z = whole(jnp.stack([keep[1], take[1]]), along_y)
    spot = jnp.stack([y, z, core]).astype(jnp.int32)
    grad_weight = place_blocks(spot, around(sum_y, along_y), around(sum_z, along_z))

    grad_context = move_blocks(returned, owner, width).reshape(slots, width)
    logit_blocks = returned[:, :, width]
    grad_logit = jnp.sum(jnp.where(match[:, :, None], logit_blocks[:, None, :], 0), axis=0).reshape(-1)
    return (update, grad_context, narrow(grad_logit), grad_weight)


def solution(mesh):
    placed = (
        P(("dp", "fsdp"), None),
        P(("dp", "fsdp")),
        P(("dp", "fsdp"), None),
        P(("dp", "fsdp"), None),
        P("fsdp", None),
        P(("dp", "fsdp"), None),
    )
    return jax.shard_map(
        on_device,
        mesh=mesh,
        in_specs=placed,
        out_specs=(
            P(("dp", "fsdp"), None),
            P(("dp", "fsdp"), None),
            P(("dp", "fsdp")),
            P("fsdp", None),
        ),
        check_vma=False,
    )
```

```python
import math

import jax
import jax.numpy as jnp
from jax import lax
from jax.experimental import pallas as pl
from jax.experimental.pallas import tpu as pltpu
from jax.sharding import PartitionSpec as P

EXTRA = 128
MIB = 1024 * 1024
NO_COST = pl.CostEstimate(flops=0, bytes_accessed=0, transcendentals=0)


def params(limit=24):
    return pltpu.CompilerParams(vmem_limit_bytes=limit * MIB)


def after(value, *others):
    return lax.optimization_barrier((value, others))[0]


def pick_body(owner_ref, listed_ref, logit_ref, head_ref, out_ref, onehot_ref, head, picked, in_sems, out_sems):
    rows, count = onehot_ref.shape
    blocks = owner_ref.shape[0]
    block = rows // blocks
    steps = in_sems.shape[0]
    width = head.shape[1]
    columns = width // steps

    def fetch(step):
        span = pl.ds(step * columns, columns)
        return pltpu.make_async_copy(head_ref.at[:, span], head.at[:, span], in_sems.at[step])

    def hand_over(step):
        span = pl.ds(step * columns, columns if step < steps else EXTRA)
        return pltpu.make_async_copy(picked.at[:, span], out_ref.at[:, span], out_sems.at[step])

    for step in range(steps):
        fetch(step).start()

    tokens = lax.broadcasted_iota(jnp.int32, (block, count), 1)
    for peer in range(rows // block):
        found = jnp.int32(blocks)
        for b in range(blocks):
            found = jnp.where(owner_ref[b] == peer, b, found)
        start = pl.multiple_of(jnp.minimum(found, blocks - 1) * block, block)
        listed = jnp.where(found < blocks, listed_ref[pl.ds(start, block), :], -1)
        onehot_ref[peer * block : (peer + 1) * block, :] = (listed == tokens).astype(jnp.bfloat16)
    first = lax.broadcasted_iota(jnp.int32, (EXTRA, count), 0) == 0
    extra = jnp.where(first, jax.nn.sigmoid(logit_ref[...]), 1.0).astype(jnp.bfloat16)
    picked[:, width:] = lax.dot_general(
        onehot_ref[...], extra, (((1,), (1,)), ((), ())), preferred_element_type=jnp.float32
    ).astype(jnp.bfloat16)
    hand_over(steps).start()
    gate = picked[:, width : width + 1].astype(jnp.float32)

    for step in range(steps):
        fetch(step).wait()
        span = slice(step * columns, (step + 1) * columns)
        rows_of_step = jnp.dot(onehot_ref[...], head[:, span], preferred_element_type=jnp.float32)
        picked[:, span] = (gate * rows_of_step).astype(jnp.bfloat16)
        hand_over(step).start()
    for step in range(steps + 1):
        hand_over(step).wait()


def pick_rows(owner, listed, logits, head):
    rows = listed.shape[0]
    count, width = head.shape
    steps = width // 512
    vmem = pl.BlockSpec(memory_space=pltpu.VMEM)
    return pl.pallas_call(
        pick_body,
        out_shape=jax.ShapeDtypeStruct((rows, width + EXTRA), jnp.bfloat16),
        in_specs=[
            pl.BlockSpec(memory_space=pltpu.SMEM),
            vmem,
            vmem,
            pl.BlockSpec(memory_space=pl.ANY),
        ],
        out_specs=pl.BlockSpec(memory_space=pl.ANY),
        scratch_shapes=[
            pltpu.VMEM((rows, count), jnp.bfloat16),
            pltpu.VMEM((count, width), jnp.bfloat16),
            pltpu.VMEM((rows, width + EXTRA), jnp.bfloat16),
            pltpu.SemaphoreType.DMA((steps,)),
            pltpu.SemaphoreType.DMA((steps + 1,)),
        ],
        compiler_params=params(56),
        cost_estimate=NO_COST,
        name="pick_rows",
    )(owner, listed, logits, head)


def move_body(width, index_ref, source_ref, out_ref):
    blocks = source_ref.shape[0]
    for slot in range(out_ref.shape[0]):
        block = index_ref[slot]

        @pl.when(block < blocks)
        def _():
            out_ref[slot] = source_ref[jnp.minimum(block, blocks - 1), :, :width]

        @pl.when(block >= blocks)
        def _():
            out_ref[slot] = jnp.zeros(out_ref.shape[1:], out_ref.dtype)


def move_blocks(source, index, width):
    blocks, rows, _ = source.shape
    copies = index.shape[0]
    return pl.pallas_call(
        lambda *refs: move_body(width, *refs),
        out_shape=jax.ShapeDtypeStruct((copies, rows, width), source.dtype),
        in_specs=[
            pl.BlockSpec(memory_space=pltpu.SMEM),
            pl.BlockSpec(memory_space=pltpu.VMEM),
        ],
        out_specs=pl.BlockSpec(memory_space=pltpu.VMEM),
        compiler_params=params(),
        cost_estimate=NO_COST,
        name="move_blocks",
    )(index, source)


def answer_body(width, slot_ref, rows_ref, weight_ref, cot_ref, back_ref, total_ref, logit_ref):
    step = pl.program_id(0)

    @pl.when(step == 0)
    def _():
        total_ref[...] = jnp.zeros_like(total_ref)

    total_ref[...] += lax.dot_general(
        cot_ref[...], weight_ref[...], (((1,), (1,)), ((), ())), preferred_element_type=jnp.float32
    )

    @pl.when(step == pl.num_programs(0) - 1)
    def _():
        gate = rows_ref[:, width : width + 1].astype(jnp.float32)
        inner = jnp.sum(rows_ref[:, :width].astype(jnp.float32) * total_ref[...], axis=1, keepdims=True)
        logit_ref[...] = jnp.broadcast_to((1.0 - gate) * inner, logit_ref.shape)
        total_ref[...] *= gate
        block = back_ref.shape[1]
        for peer in range(back_ref.shape[0]):
            here = pl.ds(pl.multiple_of(slot_ref[peer] * block, block), block)
            back_ref[peer, :, :width] = total_ref[here, :].astype(jnp.bfloat16)
            back_ref[peer, :, width:] = logit_ref[here, :].astype(jnp.bfloat16)


def answer(rows, weight, cotangent, slots, block):
    count, wide = rows.shape
    width, model = weight.shape
    columns = 1024
    return pl.pallas_call(
        lambda *refs: answer_body(width, *refs),
        out_shape=jax.ShapeDtypeStruct((slots.shape[0], block, wide), jnp.bfloat16),
        grid=(model // columns,),
        in_specs=[
            pl.BlockSpec(memory_space=pltpu.SMEM),
            pl.BlockSpec((count, wide), lambda n: (0, 0)),
            pl.BlockSpec((width, columns), lambda n: (0, n)),
            pl.BlockSpec((count, columns), lambda n: (0, n)),
        ],
        out_specs=pl.BlockSpec((slots.shape[0], block, wide), lambda n: (0, 0, 0)),
        scratch_shapes=[
            pltpu.VMEM((count, width), jnp.float32),
            pltpu.VMEM((count, EXTRA), jnp.float32),
        ],
        compiler_params=params(56),
        cost_estimate=NO_COST,
        name="answer",
    )(slots, rows, weight, cotangent)


def project_body(width, rows_ref, weight_ref, update_ref):
    gated = jnp.dot(rows_ref[:, :width], weight_ref[...], preferred_element_type=jnp.float32)
    update_ref[...] = gated.astype(jnp.bfloat16)


def project(rows, weight):
    count, wide = rows.shape
    width, model = weight.shape
    columns = 1024
    return pl.pallas_call(
        lambda *refs: project_body(width, *refs),
        out_shape=jax.ShapeDtypeStruct((count, model), jnp.bfloat16),
        grid=(model // columns,),
        in_specs=[
            pl.BlockSpec((count, wide), lambda n: (0, 0)),
            pl.BlockSpec((width, columns), lambda n: (0, n)),
        ],
        out_specs=pl.BlockSpec((count, columns), lambda n: (0, n)),
        compiler_params=params(56),
        cost_estimate=NO_COST,
        name="project",
    )(rows, weight)


def place_body(side, which, spot_ref, *refs):
    out_ref = refs[-1]
    columns = refs[0].shape[2]
    for ahead in range(side):
        left = (spot_ref[which] - ahead + side) % side * columns
        out_ref[:, pl.ds(pl.multiple_of(left, columns), columns)] = refs[ahead][0].astype(jnp.float32)


def place_blocks(which, spot, pieces, whole=None):
    side = len(pieces)
    halves, rows, columns = pieces[0].shape
    block = pl.BlockSpec((1, rows, columns), lambda h, spot_ref: (h, 0, 0))
    rest = () if whole is None else (whole,)
    return pl.pallas_call(
        lambda *refs: place_body(side, which, *refs),
        out_shape=jax.ShapeDtypeStruct((rows, halves * 2 * side * columns), jnp.float32),
        grid_spec=pltpu.PrefetchScalarGridSpec(
            num_scalar_prefetch=1,
            grid=(halves,),
            in_specs=[block] * side + [pl.BlockSpec(memory_space=pl.ANY)] * len(rest),
            out_specs=pl.BlockSpec(
                (rows, side * columns), lambda h, spot_ref: (0, (h + spot_ref[2]) % halves * 2 + which)
            ),
        ),
        input_output_aliases={1 + side: 0} if rest else {},
        compiler_params=params(),
        cost_estimate=NO_COST,
        name="place_blocks",
    )(spot, *pieces, *rest)


def at(array, index, axis=0):
    return lax.dynamic_index_in_dim(array, index, axis, keepdims=False)


def on_device(head_output, router_logits, chosen_slots, block_owner, out_weight, cotangent):
    n_dp, n_fsdp = lax.axis_size("dp"), lax.axis_size("fsdp")
    dp, fsdp = lax.axis_index("dp"), lax.axis_index("fsdp")
    side, chips = math.isqrt(n_dp), n_fsdp // 2
    y, z = dp // side, dp % side
    chip, core = fsdp // 2, fsdp % 2

    def along_x(value, ahead):
        return lax.ppermute(value, "fsdp", [(f, (f + 2 * ahead) % n_fsdp) for f in range(n_fsdp)])

    def along_y(value, ahead):
        return lax.ppermute(value, "dp", [(d, (d + side * ahead) % n_dp) for d in range(n_dp)])

    def along_z(value, ahead):
        return lax.ppermute(
            value, "dp", [(d, d // side * side + (d + ahead) % side) for d in range(n_dp)]
        )

    def to_partner(value):
        return lax.ppermute(value, "fsdp", [(f, f ^ 1) for f in range(n_fsdp)])

    slots = chosen_slots.shape[1]
    blocks = block_owner.shape[1]
    block = slots // blocks
    tokens, width = head_output.shape
    shard, model = out_weight.shape
    rows = cotangent.shape[0]
    receive = rows // block
    scale = 1.0 / math.sqrt(rows * n_dp * n_fsdp)
    half = model // 2
    owner = block_owner[0]

    weight = lax.all_gather(out_weight, "fsdp", axis=0, tiled=True)

    own_cot = lax.dynamic_slice(cotangent, (0, core * half), (rows, half))
    partner_cot = to_partner(lax.dynamic_slice(cotangent, (0, (1 - core) * half), (rows, half)))

    peers = jnp.arange(n_dp, dtype=jnp.int32)
    match = owner[None, :] == peers[:, None]
    send = pick_rows(owner, chosen_slots.reshape(slots, 1), router_logits.reshape(1, tokens), head_output)
    send = send.reshape(n_dp, block, width + EXTRA)
    got = lax.all_to_all(send, "dp", split_axis=0, concat_axis=0, tiled=True)

    both_cot = jnp.concatenate([own_cot, partner_cot], axis=0)
    got, both_cot = lax.optimization_barrier((got, both_cot))
    incoming = (got[:, 0, width + 1] > 0.5).astype(jnp.int32)
    position = jnp.cumsum(incoming) - 1
    ids = jnp.arange(receive, dtype=jnp.int32)
    source = jnp.sum(
        jnp.where((position[None, :] == ids[:, None]) & (incoming[None, :] > 0), peers[None, :], 0),
        axis=1,
    )
    held = move_blocks(got, source, width + EXTRA).reshape(rows, width + EXTRA)

    both = jnp.concatenate([held, to_partner(held)], axis=0)
    both_rows = both[:, :width]
    part = half // (2 * side)

    def term(first, index):
        columns = lax.dynamic_slice(both_cot, (0, first + index % side * part), (2 * rows, part))
        product = lax.dot_general(
            both_rows, columns, (((0,), (0,)), ((), ())), preferred_element_type=jnp.float32
        )
        return product * scale

    def wide(value):
        return value.astype(jnp.float32)

    def narrow(value):
        return value.astype(jnp.bfloat16)

    cut = width // 2
    far_y, far_z = narrow(term(0, y + 2)), narrow(term(half // 2, z + 2))
    got_parts = (
        along_y(far_y[:cut], 1), along_z(far_z[:cut], 1), along_y(far_y[cut:], -1), along_z(far_z[cut:], -1)
    )
    ahead_y, ahead_z = narrow(term(0, y + 1)), narrow(term(half // 2, z + 1))
    behind_y, behind_z = narrow(term(0, y + side - 1)), narrow(term(half // 2, z + side - 1))
    own_y, own_z = narrow(term(0, y)), narrow(term(half // 2, z))
    got_parts = after(got_parts, ahead_y, ahead_z, behind_y, behind_z, own_y, own_z)
    low_y, low_z, high_y, high_z = [wide(part_sum) for part_sum in got_parts]
    sent = (
        narrow(jnp.concatenate([wide(ahead_y[:cut]) + low_y, wide(ahead_y[cut:])], axis=0)),
        narrow(jnp.concatenate([wide(ahead_z[:cut]) + low_z, wide(ahead_z[cut:])], axis=0)),
        narrow(jnp.concatenate([wide(behind_y[:cut]), wide(behind_y[cut:]) + high_y], axis=0)),
        narrow(jnp.concatenate([wide(behind_z[:cut]), wide(behind_z[cut:]) + high_z], axis=0)),
    )
    from_y, from_z = along_y(sent[0], 1), along_z(sent[1], 1)
    to_y, to_z = along_y(sent[2], -1), along_z(sent[3], -1)

    slot = after(jnp.clip(position, 0, receive - 1), sent)
    back = answer(held, weight, cotangent, slot, block)
    returned = lax.all_to_all(back, "dp", split_axis=0, concat_axis=0, tiled=True)
    from_y, to_y, from_z, to_z = after((from_y, to_y, from_z, to_z), back)

    def rows_of(ahead):
        start = (chip + ahead) % chips * (2 * shard)

        def cut_out(value):
            return wide(lax.dynamic_slice(value, (start, 0), (2 * shard, part)))

        return jnp.stack(
            [
                cut_out(own) + cut_out(up) + cut_out(down)
                for own, up, down in ((own_y, from_y, to_y), (own_z, from_z, to_z))
            ]
        )

    order = [2, 1] + list(range(3, chips))
    chunks = [narrow(rows_of(ahead)) for ahead in order]
    terms = [rows_of(0)] + [along_x(chunk, ahead) for chunk, ahead in zip(chunks, order)]
    update = project(after(held, *chunks), weight)
    terms = after(terms, returned, update)

    def rows_for(which):
        total = sum(wide(at(term_x.reshape(2, 2, shard, part), which, 1)) for term_x in terms)
        return narrow(total)

    take = to_partner(rows_for(1 - core))
    keep = rows_for(core)

    def around(value, along):
        return [value] + [along(value, ahead) for ahead in range(1, side)]

    def whole(value, along):
        values = [wide(one) for one in around(value, along)]
        return narrow((values[0] + values[2]) + (values[1] + values[3]))

    sum_y = whole(jnp.stack([keep[0], take[0]]), along_z)
    sum_z = whole(jnp.stack([keep[1], take[1]]), along_y)
    spot = jnp.stack([y, z, core]).astype(jnp.int32)
    grad_weight = place_blocks(0, spot, around(sum_y, along_y))
    grad_weight = place_blocks(1, spot, around(sum_z, along_z), grad_weight)

    grad_context = move_blocks(returned, owner, width).reshape(slots, width)
    logit_blocks = returned[:, :, width]
    grad_logit = jnp.sum(jnp.where(match[:, :, None], logit_blocks[:, None, :], 0), axis=0).reshape(-1)
    return (update, grad_context, narrow(grad_logit), grad_weight)


def solution(mesh):
    placed = (
        P(("dp", "fsdp"), None),
        P(("dp", "fsdp")),
        P(("dp", "fsdp"), None),
        P(("dp", "fsdp"), None),
        P("fsdp", None),
        P(("dp", "fsdp"), None),
    )
    return jax.shard_map(
        on_device,
        mesh=mesh,
        in_specs=placed,
        out_specs=(
            P(("dp", "fsdp"), None),
            P(("dp", "fsdp"), None),
            P(("dp", "fsdp")),
            P("fsdp", None),
        ),
        check_vma=False,
    )
```

```python
import math

import jax
import jax.numpy as jnp
from jax import lax
from jax.experimental import pallas as pl
from jax.experimental.pallas import tpu as pltpu
from jax.sharding import PartitionSpec as P

EXTRA = 128
MIB = 1024 * 1024
NO_COST = pl.CostEstimate(flops=0, bytes_accessed=0, transcendentals=0)


def params(limit=24):
    return pltpu.CompilerParams(vmem_limit_bytes=limit * MIB)


def after(value, *others):
    return lax.optimization_barrier((value, others))[0]


def pick_body(owner_ref, listed_ref, logit_ref, head_ref, out_ref, onehot_ref, head, picked, in_sems, out_sems):
    rows, count = onehot_ref.shape
    blocks = owner_ref.shape[0]
    block = rows // blocks
    steps = in_sems.shape[0]
    width = head.shape[1]
    columns = width // steps

    def fetch(step):
        span = pl.ds(step * columns, columns)
        return pltpu.make_async_copy(head_ref.at[:, span], head.at[:, span], in_sems.at[step])

    def hand_over(step):
        span = pl.ds(step * columns, columns if step < steps else EXTRA)
        return pltpu.make_async_copy(picked.at[:, span], out_ref.at[:, span], out_sems.at[step])

    for step in range(steps):
        fetch(step).start()

    tokens = lax.broadcasted_iota(jnp.int32, (block, count), 1)
    for peer in range(rows // block):
        found = jnp.int32(blocks)
        for b in range(blocks):
            found = jnp.where(owner_ref[b] == peer, b, found)
        start = pl.multiple_of(jnp.minimum(found, blocks - 1) * block, block)
        listed = jnp.where(found < blocks, listed_ref[pl.ds(start, block), :], -1)
        onehot_ref[peer * block : (peer + 1) * block, :] = (listed == tokens).astype(jnp.bfloat16)
    first = lax.broadcasted_iota(jnp.int32, (EXTRA, count), 0) == 0
    extra = jnp.where(first, jax.nn.sigmoid(logit_ref[...]), 1.0).astype(jnp.bfloat16)
    picked[:, width:] = lax.dot_general(
        onehot_ref[...], extra, (((1,), (1,)), ((), ())), preferred_element_type=jnp.float32
    ).astype(jnp.bfloat16)
    hand_over(steps).start()
    gate = picked[:, width : width + 1].astype(jnp.float32)

    for step in range(steps):
        fetch(step).wait()
        span = slice(step * columns, (step + 1) * columns)
        rows_of_step = jnp.dot(onehot_ref[...], head[:, span], preferred_element_type=jnp.float32)
        picked[:, span] = (gate * rows_of_step).astype(jnp.bfloat16)
        hand_over(step).start()
    for step in range(steps + 1):
        hand_over(step).wait()


def pick_rows(owner, listed, logits, head):
    rows = listed.shape[0]
    count, width = head.shape
    steps = width // 512
    vmem = pl.BlockSpec(memory_space=pltpu.VMEM)
    return pl.pallas_call(
        pick_body,
        out_shape=jax.ShapeDtypeStruct((rows, width + EXTRA), jnp.bfloat16),
        in_specs=[
            pl.BlockSpec(memory_space=pltpu.SMEM),
            vmem,
            vmem,
            pl.BlockSpec(memory_space=pl.ANY),
        ],
        out_specs=pl.BlockSpec(memory_space=pl.ANY),
        scratch_shapes=[
            pltpu.VMEM((rows, count), jnp.bfloat16),
            pltpu.VMEM((count, width), jnp.bfloat16),
            pltpu.VMEM((rows, width + EXTRA), jnp.bfloat16),
            pltpu.SemaphoreType.DMA((steps,)),
            pltpu.SemaphoreType.DMA((steps + 1,)),
        ],
        compiler_params=params(56),
        cost_estimate=NO_COST,
        name="pick_rows",
    )(owner, listed, logits, head)


def move_body(width, index_ref, source_ref, out_ref):
    blocks = source_ref.shape[0]
    for slot in range(out_ref.shape[0]):
        block = index_ref[slot]

        @pl.when(block < blocks)
        def _():
            out_ref[slot] = source_ref[jnp.minimum(block, blocks - 1), :, :width]

        @pl.when(block >= blocks)
        def _():
            out_ref[slot] = jnp.zeros(out_ref.shape[1:], out_ref.dtype)


def move_blocks(source, index, width):
    blocks, rows, _ = source.shape
    copies = index.shape[0]
    return pl.pallas_call(
        lambda *refs: move_body(width, *refs),
        out_shape=jax.ShapeDtypeStruct((copies, rows, width), source.dtype),
        in_specs=[
            pl.BlockSpec(memory_space=pltpu.SMEM),
            pl.BlockSpec(memory_space=pltpu.VMEM),
        ],
        out_specs=pl.BlockSpec(memory_space=pltpu.VMEM),
        compiler_params=params(),
        cost_estimate=NO_COST,
        name="move_blocks",
    )(index, source)


def answer_body(width, slot_ref, rows_ref, weight_ref, cot_ref, back_ref, total_ref, logit_ref):
    step = pl.program_id(0)

    @pl.when(step == 0)
    def _():
        total_ref[...] = jnp.zeros_like(total_ref)

    total_ref[...] += lax.dot_general(
        cot_ref[...], weight_ref[...], (((1,), (1,)), ((), ())), preferred_element_type=jnp.float32
    )

    @pl.when(step == pl.num_programs(0) - 1)
    def _():
        gate = rows_ref[:, width : width + 1].astype(jnp.float32)
        inner = jnp.sum(rows_ref[:, :width].astype(jnp.float32) * total_ref[...], axis=1, keepdims=True)
        logit_ref[...] = jnp.broadcast_to((1.0 - gate) * inner, logit_ref.shape)
        total_ref[...] *= gate
        block = back_ref.shape[1]
        for peer in range(back_ref.shape[0]):
            here = pl.ds(pl.multiple_of(slot_ref[peer] * block, block), block)
            back_ref[peer, :, :width] = total_ref[here, :].astype(jnp.bfloat16)
            back_ref[peer, :, width:] = logit_ref[here, :].astype(jnp.bfloat16)


def answer(rows, weight, cotangent, slots, block):
    count, wide = rows.shape
    width, model = weight.shape
    columns = 1024
    return pl.pallas_call(
        lambda *refs: answer_body(width, *refs),
        out_shape=jax.ShapeDtypeStruct((slots.shape[0], block, wide), jnp.bfloat16),
        grid=(model // columns,),
        in_specs=[
            pl.BlockSpec(memory_space=pltpu.SMEM),
            pl.BlockSpec((count, wide), lambda n: (0, 0)),
            pl.BlockSpec((width, columns), lambda n: (0, n)),
            pl.BlockSpec((count, columns), lambda n: (0, n)),
        ],
        out_specs=pl.BlockSpec((slots.shape[0], block, wide), lambda n: (0, 0, 0)),
        scratch_shapes=[
            pltpu.VMEM((count, width), jnp.float32),
            pltpu.VMEM((count, EXTRA), jnp.float32),
        ],
        compiler_params=params(56),
        cost_estimate=NO_COST,
        name="answer",
    )(slots, rows, weight, cotangent)


def project_body(width, rows_ref, weight_ref, update_ref):
    gated = jnp.dot(rows_ref[:, :width], weight_ref[...], preferred_element_type=jnp.float32)
    update_ref[...] = gated.astype(jnp.bfloat16)


def project(rows, weight):
    count, wide = rows.shape
    width, model = weight.shape
    columns = 1024
    return pl.pallas_call(
        lambda *refs: project_body(width, *refs),
        out_shape=jax.ShapeDtypeStruct((count, model), jnp.bfloat16),
        grid=(model // columns,),
        in_specs=[
            pl.BlockSpec((count, wide), lambda n: (0, 0)),
            pl.BlockSpec((width, columns), lambda n: (0, n)),
        ],
        out_specs=pl.BlockSpec((count, columns), lambda n: (0, n)),
        compiler_params=params(56),
        cost_estimate=NO_COST,
        name="project",
    )(rows, weight)


def place_body(side, which, spot_ref, *refs):
    out_ref = refs[-1]
    columns = refs[0].shape[2]
    for ahead in range(side):
        left = (spot_ref[which] - ahead + side) % side * columns
        out_ref[:, pl.ds(pl.multiple_of(left, columns), columns)] = refs[ahead][0].astype(jnp.float32)


def place_blocks(which, spot, pieces, whole=None):
    side = len(pieces)
    halves, rows, columns = pieces[0].shape
    block = pl.BlockSpec((1, rows, columns), lambda h, spot_ref: (h, 0, 0))
    rest = () if whole is None else (whole,)
    return pl.pallas_call(
        lambda *refs: place_body(side, which, *refs),
        out_shape=jax.ShapeDtypeStruct((rows, halves * 2 * side * columns), jnp.float32),
        grid_spec=pltpu.PrefetchScalarGridSpec(
            num_scalar_prefetch=1,
            grid=(halves,),
            in_specs=[block] * side + [pl.BlockSpec(memory_space=pl.ANY)] * len(rest),
            out_specs=pl.BlockSpec(
                (rows, side * columns), lambda h, spot_ref: (0, (h + spot_ref[2]) % halves * 2 + which)
            ),
        ),
        input_output_aliases={1 + side: 0} if rest else {},
        compiler_params=params(),
        cost_estimate=NO_COST,
        name="place_blocks",
    )(spot, *pieces, *rest)


def at(array, index, axis=0):
    return lax.dynamic_index_in_dim(array, index, axis, keepdims=False)


def on_device(head_output, router_logits, chosen_slots, block_owner, out_weight, cotangent):
    n_dp, n_fsdp = lax.axis_size("dp"), lax.axis_size("fsdp")
    dp, fsdp = lax.axis_index("dp"), lax.axis_index("fsdp")
    side, chips = math.isqrt(n_dp), n_fsdp // 2
    y, z = dp // side, dp % side
    chip, core = fsdp // 2, fsdp % 2

    def along_x(value, ahead):
        return lax.ppermute(value, "fsdp", [(f, (f + 2 * ahead) % n_fsdp) for f in range(n_fsdp)])

    def along_y(value, ahead):
        return lax.ppermute(value, "dp", [(d, (d + side * ahead) % n_dp) for d in range(n_dp)])

    def along_z(value, ahead):
        return lax.ppermute(
            value, "dp", [(d, d // side * side + (d + ahead) % side) for d in range(n_dp)]
        )

    def to_partner(value):
        return lax.ppermute(value, "fsdp", [(f, f ^ 1) for f in range(n_fsdp)])

    slots = chosen_slots.shape[1]
    blocks = block_owner.shape[1]
    block = slots // blocks
    tokens, width = head_output.shape
    shard, model = out_weight.shape
    rows = cotangent.shape[0]
    receive = rows // block
    scale = 1.0 / math.sqrt(rows * n_dp * n_fsdp)
    half = model // 2
    owner = block_owner[0]

    weight = lax.all_gather(out_weight, "fsdp", axis=0, tiled=True)

    own_cot = lax.dynamic_slice(cotangent, (0, core * half), (rows, half))
    partner_cot = to_partner(lax.dynamic_slice(cotangent, (0, (1 - core) * half), (rows, half)))

    peers = jnp.arange(n_dp, dtype=jnp.int32)
    match = owner[None, :] == peers[:, None]
    send = pick_rows(owner, chosen_slots.reshape(slots, 1), router_logits.reshape(1, tokens), head_output)
    send = send.reshape(n_dp, block, width + EXTRA)
    got = lax.all_to_all(send, "dp", split_axis=0, concat_axis=0, tiled=True)

    both_cot = jnp.concatenate([own_cot, partner_cot], axis=0)
    got, both_cot = lax.optimization_barrier((got, both_cot))
    incoming = (got[:, 0, width + 1] > 0.5).astype(jnp.int32)
    position = jnp.cumsum(incoming) - 1
    ids = jnp.arange(receive, dtype=jnp.int32)
    source = jnp.sum(
        jnp.where((position[None, :] == ids[:, None]) & (incoming[None, :] > 0), peers[None, :], 0),
        axis=1,
    )
    held = move_blocks(got, source, width + EXTRA).reshape(rows, width + EXTRA)

    both = jnp.concatenate([held, to_partner(held)], axis=0)
    both_rows = both[:, :width]
    part = half // (2 * side)

    def term(first, index):
        columns = lax.dynamic_slice(both_cot, (0, first + index % side * part), (2 * rows, part))
        product = lax.dot_general(
            both_rows, columns, (((0,), (0,)), ((), ())), preferred_element_type=jnp.float32
        )
        return product * scale

    def wide(value):
        return value.astype(jnp.float32)

    def narrow(value):
        return value.astype(jnp.bfloat16)

    cut = width // 2
    far_y, far_z = narrow(term(0, y + 2)), narrow(term(half // 2, z + 2))
    got_parts = (
        along_y(far_y[:cut], 1), along_z(far_z[:cut], 1), along_y(far_y[cut:], -1), along_z(far_z[cut:], -1)
    )
    ahead_y, ahead_z = narrow(term(0, y + 1)), narrow(term(half // 2, z + 1))
    behind_y, behind_z = narrow(term(0, y + side - 1)), narrow(term(half // 2, z + side - 1))
    own_y, own_z = narrow(term(0, y)), narrow(term(half // 2, z))
    got_parts = after(got_parts, ahead_y, ahead_z, behind_y, behind_z, own_y, own_z)
    low_y, low_z, high_y, high_z = [wide(part_sum) for part_sum in got_parts]
    sent = (
        narrow(jnp.concatenate([wide(ahead_y[:cut]) + low_y, wide(ahead_y[cut:])], axis=0)),
        narrow(jnp.concatenate([wide(ahead_z[:cut]) + low_z, wide(ahead_z[cut:])], axis=0)),
        narrow(jnp.concatenate([wide(behind_y[:cut]), wide(behind_y[cut:]) + high_y], axis=0)),
        narrow(jnp.concatenate([wide(behind_z[:cut]), wide(behind_z[cut:]) + high_z], axis=0)),
    )
    from_y, from_z = along_y(sent[0], 1), along_z(sent[1], 1)
    to_y, to_z = along_y(sent[2], -1), along_z(sent[3], -1)

    slot = after(jnp.clip(position, 0, receive - 1), sent)
    back = answer(held, weight, cotangent, slot, block)
    returned = lax.all_to_all(back, "dp", split_axis=0, concat_axis=0, tiled=True)
    from_y, to_y, from_z, to_z = after((from_y, to_y, from_z, to_z), back)

    def rows_of(ahead):
        start = (chip + ahead) % chips * (2 * shard)

        def cut_out(value):
            return wide(lax.dynamic_slice(value, (start, 0), (2 * shard, part)))

        return jnp.stack(
            [
                cut_out(own) + cut_out(up) + cut_out(down)
                for own, up, down in ((own_y, from_y, to_y), (own_z, from_z, to_z))
            ]
        )

    order = [2, 1] + list(range(3, chips))
    chunks = [narrow(rows_of(ahead)) for ahead in order]
    terms = [rows_of(0)] + [along_x(chunk, ahead) for chunk, ahead in zip(chunks, order)]
    update = project(after(held, *chunks), weight)
    terms = after(terms, returned, update)

    def rows_for(which):
        total = sum(wide(at(term_x.reshape(2, 2, shard, part), which, 1)) for term_x in terms)
        return narrow(total)

    take = to_partner(rows_for(1 - core))
    keep = rows_for(core)

    def around(value, along):
        return [value] + [along(value, ahead) for ahead in range(1, side)]

    def whole(value, beside, along):
        pair = narrow(wide(value) + wide(beside(value)))
        return narrow(wide(pair) + wide(along(pair, 2)))

    def beside_y(value):
        return lax.ppermute(value, "dp", [(d, d ^ side) for d in range(n_dp)])

    def beside_z(value):
        return lax.ppermute(value, "dp", [(d, d ^ 1) for d in range(n_dp)])

    sum_y = whole(jnp.stack([keep[0], take[0]]), beside_z, along_z)
    sum_z = whole(jnp.stack([keep[1], take[1]]), beside_y, along_y)
    spot = jnp.stack([y, z, core]).astype(jnp.int32)
    grad_weight = place_blocks(0, spot, around(sum_y, along_y))
    grad_weight = place_blocks(1, spot, around(sum_z, along_z), grad_weight)

    grad_context = move_blocks(returned, owner, width).reshape(slots, width)
    logit_blocks = returned[:, :, width]
    grad_logit = jnp.sum(jnp.where(match[:, :, None], logit_blocks[:, None, :], 0), axis=0).reshape(-1)
    return (update, grad_context, narrow(grad_logit), grad_weight)


def solution(mesh):
    placed = (
        P(("dp", "fsdp"), None),
        P(("dp", "fsdp")),
        P(("dp", "fsdp"), None),
        P(("dp", "fsdp"), None),
        P("fsdp", None),
        P(("dp", "fsdp"), None),
    )
    return jax.shard_map(
        on_device,
        mesh=mesh,
        in_specs=placed,
        out_specs=(
            P(("dp", "fsdp"), None),
            P(("dp", "fsdp"), None),
            P(("dp", "fsdp")),
            P("fsdp", None),
        ),
        check_vma=False,
    )
```
